32 devices in a mesh: outer: 8 (over z, x), inner: 4 (over y, core).
Axes of the slice: x: 2, y: 2, z: 4, core: 2. Of those that a mesh axis runs over, the one named last changes fastest.
Arguments:
- queries: bfloat16 [2048, 2048], P(('outer', 'inner')), may hold values from -32 to 32
- keys: bfloat16 [2048, 2048], P(('outer', 'inner')), may hold values from -8 to 8
- values: bfloat16 [2048, 2048], P(('outer', 'inner')), may hold values from -24 to 24
- span_order: int32 [64], P(('outer', 'inner')), may hold values from 0 to 63, each once
Outputs:
- attended: bfloat16 [2048, 2048], P(('outer', 'inner'))
- log_total: float32 [16, 2048], P(None, ('outer', 'inner'))
The draws below stay inside these ranges and needn't reach their ends.
Inputs may be any that keep to these rules, and one draw needn't show every extreme that they name: `span_order`: a permutation of the span ranks, so positions is a permutation of the rows in which each span of 32 rows holds consecutive ranks in row order.
All inputs are finite; a program needn't handle non-finite values.
Results may differ from the reference program's by a relative error of at most 0.0065.
Values may be sent and summed in bfloat16 or wider, within the bound.
No kernel may reach another device: no remote copies, remote signals or barrier semaphores. Data moves between devices by JAX's collectives and lax.ppermute only.
A program may use at most 64 MiB of HBM per device.

```python
import math
import jax
import jax.numpy as jnp
from jax import lax

HEADS = 16
HEAD_DIM = 128
MODEL = 2048
SPAN = 32
TOKENS = 2048


def shared_keys(key):
    key_normal = jax.random.fold_in(jax.random.fold_in(key, 7), 0)
    normal = jnp.clip(jax.random.normal(key_normal, (TOKENS, MODEL), jnp.float32), -5.0, 5.0)
    return normal


def draw_keys(key, part):
    normal = shared_keys(key)
    return (1.5 * normal).astype(jnp.bfloat16)


def draw_queries(key, part):
    key = jax.random.fold_in(key, 2)
    own_normal = jnp.clip(jax.random.normal(key, (TOKENS, MODEL), jnp.float32), -5.0, 5.0)
    return (1.5 * own_normal).astype(jnp.bfloat16)


def block_levels(stream_key, dims, shards, least, high):
    def one(axis_at, blocks):
        heights = jax.random.uniform(jax.random.fold_in(jax.random.fold_in(stream_key, 6), axis_at), (blocks,), jnp.float32, least / len(shards), high / len(shards))
        return jnp.repeat(jnp.exp(heights), dims[axis_at] // blocks).reshape((-1,) + (1,) * (len(dims) - axis_at - 1))

    level = one(*shards[0])
    for cut in shards[1:]:
        level = level * one(*cut)
    return level


def gaussian(stream_key, shape, deviation, reach, shards=(), kind=jnp.bfloat16):
    level = block_levels(stream_key, shape, shards, -0.22, 0.18) if shards else 1.0
    result = jax.random.normal(stream_key, shape, jnp.float32) * deviation * level
    return jnp.minimum(jnp.maximum(result, -reach), reach).astype(kind)


def setup_inputs(seed: int = 0) -> dict:
    seeds = jax.random.split(jax.random.key(seed), 5)
    queries = draw_queries(jax.random.fold_in(seeds[4], 71), 0)
    keys = draw_keys(jax.random.fold_in(seeds[4], 71), 0)
    values = gaussian(seeds[2], (TOKENS, MODEL), 4.0, 24.0, ((0, 32),))
    span_order = jax.random.permutation(seeds[3], TOKENS // SPAN).astype(jnp.int32)
    return dict(queries=queries, keys=keys, values=values, span_order=span_order)


masked_score = -1e+30

def reference(queries, keys, values, span_order):
    tok_total = queries.shape[0]
    offsets = jnp.arange(SPAN, dtype=jnp.int32)
    positions = (span_order[:, None] * SPAN + offsets[None, :]).reshape(tok_total).astype(jnp.int32)
    key_heads = keys.astype(jnp.float32).reshape(tok_total, HEADS, HEAD_DIM)
    value_heads = values.astype(jnp.float32).reshape(tok_total, HEADS, HEAD_DIM)
    block_rows = math.gcd(tok_total, 256)

    def query_block(block_index):
        start = (block_index * block_rows).astype(jnp.int32)
        query_heads = lax.dynamic_slice_in_dim(queries, start, block_rows, 0).astype(jnp.float32).reshape(block_rows, HEADS, HEAD_DIM)
        query_pos = lax.dynamic_slice_in_dim(positions, start, block_rows, 0)
        scores = jnp.einsum('qhd,khd->hqk', query_heads, key_heads) * (1.0 / math.sqrt(HEAD_DIM))
        visible = positions[None, None, :] <= query_pos[None, :, None]
        scores = jnp.where(visible, scores, masked_score)
        row_max = lax.optimization_barrier(jnp.max(scores, axis=2))
        exponent = jnp.where(visible, jnp.exp(scores - row_max[:, :, None]), 0.0)
        total = lax.optimization_barrier(jnp.sum(exponent, axis=2))
        weights = exponent.astype(jnp.bfloat16).astype(jnp.float32)
        summed = jnp.einsum('hqk,khd->qhd', weights, value_heads)
        attended = (summed / jnp.transpose(total)[:, :, None]).reshape(block_rows, HEADS * HEAD_DIM).astype(jnp.bfloat16)
        return (attended, row_max + jnp.log(total))
    attended, log_total = lax.map(query_block, jnp.arange(tok_total // block_rows, dtype=jnp.int32))
    attended = attended.reshape(tok_total, HEADS * HEAD_DIM)
    log_total = jnp.transpose(log_total, (1, 0, 2)).reshape(HEADS, tok_total)
    return (attended, log_total)
```

```python
import functools
import math

import jax
import jax.numpy as jnp
from jax import lax
from jax.experimental import pallas as pl
from jax.experimental.pallas import tpu as pltpu
from jax.sharding import Mesh
from jax.sharding import PartitionSpec as P

HEADS = 16
HEAD_DIM = 128
SPAN = 32
DIGIT = 64
ROWS_PER_SPAN_PAIR = 2 * SPAN
EXTRA = 8
MASKED = -1e30
SCALE = 1.0 / math.sqrt(HEAD_DIM)
LOG2E = math.log2(math.e)
VMEM_LIMIT = 48 * 1024 * 1024


def pack_kernel(span_ref, half_ref, q_ref, k_ref, v_ref, out_ref):
    rows = q_ref.shape[0]
    for head in range(HEADS):
        lanes = slice(head * HEAD_DIM, (head + 1) * HEAD_DIM)
        out_ref[head, 0:rows, :] = q_ref[:, lanes]
        out_ref[head, rows : 2 * rows, :] = k_ref[:, lanes]
        out_ref[head, 2 * rows : 3 * rows, :] = v_ref[:, lanes]
    lane = lax.broadcasted_iota(jnp.int32, (EXTRA, HEAD_DIM), 1)
    row = lax.broadcasted_iota(jnp.int32, (EXTRA, HEAD_DIM), 0)
    local = lane - half_ref[0] * rows
    rank = jnp.where(local < SPAN, span_ref[0], span_ref[1])
    digit = jnp.where(row == 0, rank // DIGIT, rank % DIGIT)
    mine = (local >= 0) & (local < rows) & (row < 2)
    extra = jnp.where(mine, digit, 0).astype(jnp.float32).astype(jnp.bfloat16)
    for head in range(HEADS):
        out_ref[head, 3 * rows : 3 * rows + EXTRA, :] = extra


def positions(ref, rows):
    extra = ref[:, 3 * rows : 3 * rows + EXTRA, :].astype(jnp.float32)
    rank = extra[:, 0, :] * DIGIT + extra[:, 1, :]
    rank = jnp.sum(rank.reshape(HEADS // 2, 2, HEAD_DIM), axis=1)
    lane = lax.broadcasted_iota(jnp.int32, (HEADS // 2, HEAD_DIM), 1)
    return rank * SPAN + (lane % SPAN).astype(jnp.float32)


def step_kernel(first, last, *refs):
    if first:
        mine_ref, other_ref, *outs = refs
    else:
        mine_ref, other_ref, acc_in, stat_in, *outs = refs
    rows = (mine_ref.shape[1] - EXTRA) // 3
    total_rows = HEADS * rows
    query_pos = jnp.transpose(
        jnp.concatenate([positions(mine_ref, rows)] * (HEAD_DIM // (HEADS // 2)), axis=0)
    )
    key_pos = positions(other_ref, rows)
    keys = other_ref[:, rows : 2 * rows, :].reshape(total_rows, HEAD_DIM)
    values = other_ref[:, 2 * rows : 3 * rows, :].reshape(total_rows, HEAD_DIM)
    key_row = jnp.concatenate([key_pos[i : i + 1, :] for i in range(HEADS // 2)], axis=1)
    group = 4
    block = group * rows
    for index in range(HEADS // group):
        queries = mine_ref[index * group : (index + 1) * group, 0:rows, :].reshape(block, HEAD_DIM)
        scores = lax.dot_general(
            queries, keys, (((1,), (1,)), ((), ())), preferred_element_type=jnp.float32
        )
        per = block // HEAD_DIM
        query_col = jnp.concatenate(
            [query_pos[:, index * per + i : index * per + i + 1] for i in range(per)], axis=0
        )
        scores = jnp.where(key_row <= query_col, scores, MASKED)
        top = jnp.max(scores, axis=1, keepdims=True)
        here = slice(index * block, (index + 1) * block)
        if not first:
            old_top = stat_in[here, 0:1]
            top = jnp.maximum(top, old_top)
        weights = jnp.exp2((scores - top) * (SCALE * LOG2E))
        total = jnp.sum(weights, axis=1, keepdims=True)
        acc = jnp.dot(weights.astype(jnp.bfloat16), values, preferred_element_type=jnp.float32)
        if not first:
            factor = jnp.exp2((old_top - top) * (SCALE * LOG2E))
            total = total + stat_in[here, 1:2] * factor
            acc = acc + acc_in[here, :] * factor
        if last:
            out_ref = outs[0]
            result = (acc * (1.0 / total)).astype(jnp.bfloat16)
            out_ref[index * group : (index + 1) * group, 0:rows, :] = result.reshape(
                group, rows, HEAD_DIM
            )
            log_total = top * SCALE + jnp.log(total)
            for i in range(per):
                piece = jnp.broadcast_to(
                    log_total[i * HEAD_DIM : (i + 1) * HEAD_DIM], (HEAD_DIM, HEAD_DIM)
                )
                piece = jnp.transpose(piece)[0:EXTRA, :]
                high = piece.astype(jnp.bfloat16).astype(jnp.float32)
                rest = piece - high
                middle = rest.astype(jnp.bfloat16).astype(jnp.float32)
                low = rest - middle
                row = lax.broadcasted_iota(jnp.int32, piece.shape, 0)
                extra = jnp.where(row == 0, high, jnp.where(row == 1, middle, low))
                extra = extra.astype(jnp.bfloat16)
                for j in range(HEAD_DIM // rows):
                    out_ref[
                        index * group + i * (HEAD_DIM // rows) + j, rows : rows + EXTRA, :
                    ] = extra
        else:
            acc_out, stat_out = outs
            acc_out[here, :] = acc
            lane = lax.broadcasted_iota(jnp.int32, (block, HEAD_DIM), 1)
            stat_out[here, :] = jnp.where(lane == 0, top, total)


def unpack_kernel(half_ref, in_ref, out_ref, log_ref):
    rows = out_ref.shape[0]
    for head in range(HEADS):
        out_ref[:, head * HEAD_DIM : (head + 1) * HEAD_DIM] = in_ref[head, 0:rows, :]
    extra = in_ref[:, rows : rows + EXTRA, :].astype(jnp.float32)
    full = extra[:, 0, :] + extra[:, 1, :] + extra[:, 2, :]
    log_ref[...] = jnp.where(half_ref[0] == 0, full[:, 0:rows], full[:, rows : 2 * rows])


VMEM = pl.BlockSpec(memory_space=pltpu.VMEM)
SMEM = pl.BlockSpec(memory_space=pltpu.SMEM)


def call(kernel, out_shape, n_scalar, n_vector, flops=0, data=1 << 20):
    outs = out_shape if isinstance(out_shape, tuple) else None
    return pl.pallas_call(
        kernel,
        out_shape=out_shape,
        in_specs=[SMEM] * n_scalar + [VMEM] * n_vector,
        out_specs=tuple(VMEM for _ in outs) if outs else VMEM,
        compiler_params=pltpu.CompilerParams(vmem_limit_bytes=VMEM_LIMIT),
        cost_estimate=pl.CostEstimate(flops=flops, bytes_accessed=data, transcendentals=0),
    )


def local(queries, keys, values, span_order):
    rows = queries.shape[0]
    parts = lax.axis_size("part")
    half = (lax.axis_index("head") % 2).astype(jnp.int32).reshape(1)
    packed = call(
        pack_kernel,
        jax.ShapeDtypeStruct((HEADS, 3 * rows + EXTRA, HEAD_DIM), jnp.bfloat16),
        2,
        3,
    )(span_order, half, queries, keys, values)
    mine = lax.all_to_all(packed, "head", 0, 0, tiled=True)
    total_rows = HEADS * rows
    work = 4 * total_rows * total_rows * HEAD_DIM
    state = ()
    other = mine
    for part in range(parts):
        first, last = part == 0, part == parts - 1
        if last:
            shape = jax.ShapeDtypeStruct((HEADS, rows + EXTRA, HEAD_DIM), jnp.bfloat16)
        else:
            shape = (jax.ShapeDtypeStruct((total_rows, HEAD_DIM), jnp.float32),) * 2
        following = (
            None
            if last
            else lax.ppermute(other, "part", [(i, (i + 1) % parts) for i in range(parts)])
        )
        state = call(
            functools.partial(step_kernel, first, last), shape, 0, 2 if first else 4, work
        )(mine, other, *state)
        other = following
    back = lax.all_to_all(state, "head", 0, 0, tiled=True)
    return call(
        unpack_kernel,
        (
            jax.ShapeDtypeStruct((rows, HEADS * HEAD_DIM), jnp.bfloat16),
            jax.ShapeDtypeStruct((HEADS, rows), jnp.float32),
        ),
        1,
        1,
    )(half, back)


def solution(mesh):
    devices = mesh.devices.reshape(HEADS, -1)
    rows = P(("head", "part"), None)
    return jax.shard_map(
        local,
        mesh=Mesh(devices, ("head", "part")),
        in_specs=(rows, rows, rows, P(("head", "part"))),
        out_specs=(rows, P(None, ("head", "part"))),
        check_vma=False,
    )
```

```python
import functools
import math

import jax
import jax.numpy as jnp
from jax import lax
from jax.experimental import pallas as pl
from jax.experimental.pallas import tpu as pltpu
from jax.sharding import Mesh
from jax.sharding import PartitionSpec as P

HEADS = 16
HEAD_DIM = 128
SPAN = 32
DIGIT = 64
EXTRA = 8
GROUP = 4
MASKED = -1e30
SCALE = 1.0 / math.sqrt(HEAD_DIM)
SCALE2 = SCALE * math.log2(math.e)
VMEM_LIMIT = 48 * 1024 * 1024

VMEM = pl.BlockSpec(memory_space=pltpu.VMEM)
HBM = pl.BlockSpec(memory_space=pltpu.HBM)


def pack_kernel(span_hbm, q_hbm, k_hbm, v_hbm, out_ref, span, buffers, sems):
    rows = q_hbm.shape[0]
    span_copy = pltpu.make_async_copy(span_hbm, span, sems.at[3])
    span_copy.start()
    copies = [
        pltpu.make_async_copy(source, buffers.at[i], sems.at[i])
        for i, source in enumerate((q_hbm, k_hbm, v_hbm))
    ]
    for copy in copies:
        copy.start()
    span_copy.wait()
    lane = lax.broadcasted_iota(jnp.int32, (EXTRA, HEAD_DIM), 1)
    row = lax.broadcasted_iota(jnp.int32, (EXTRA, HEAD_DIM), 0)
    local = lane - (lax.axis_index("head") % 2) * rows
    rank = jnp.where(local < SPAN, span[0], span[1])
    digit = jnp.where(row == 0, rank // DIGIT, rank % DIGIT)
    mine = (local >= 0) & (local < rows) & (row < 2)
    extra = jnp.where(mine, digit, 0).astype(jnp.float32).astype(jnp.bfloat16)
    for head in range(HEADS):
        out_ref[head, 3 * rows : 3 * rows + EXTRA, :] = extra
    for i, copy in enumerate(copies):
        copy.wait()
        for head in range(HEADS):
            out_ref[head, i * rows : (i + 1) * rows, :] = buffers[
                i, :, head * HEAD_DIM : (head + 1) * HEAD_DIM
            ]


def positions(ref, rows):
    extra = ref[:, 3 * rows : 3 * rows + EXTRA, :].astype(jnp.float32)
    rank = extra[:, 0, :] * DIGIT + extra[:, 1, :]
    rank = jnp.sum(rank.reshape(HEADS // 2, 2, HEAD_DIM), axis=1)
    lane = lax.broadcasted_iota(jnp.int32, (HEADS // 2, HEAD_DIM), 1)
    return rank * SPAN + (lane % SPAN).astype(jnp.float32)


def attend_kernel(first, last, mine_ref, other_ref, *refs):
    if first:
        outs = refs
    else:
        acc_in, total_in, top_in, *outs = refs
    rows = (mine_ref.shape[1] - EXTRA) // 3
    keys_total = HEADS * rows
    block = GROUP * rows
    blocks = HEADS // GROUP
    tiles = block // HEAD_DIM
    keys = other_ref[:, rows : 2 * rows, :].reshape(keys_total, HEAD_DIM)

    def score(index):
        queries = mine_ref[index * GROUP : (index + 1) * GROUP, 0:rows, :]
        return lax.dot_general(
            queries.reshape(block, HEAD_DIM),
            keys,
            (((1,), (1,)), ((), ())),
            preferred_element_type=jnp.float32,
        )

    next_scores = score(0)
    repeat = HEAD_DIM // (HEADS // 2)
    query_pos = jnp.transpose(jnp.concatenate([positions(mine_ref, rows)] * repeat, axis=0))
    key_pos = positions(other_ref, rows)
    key_row = jnp.concatenate([key_pos[i : i + 1, :] for i in range(HEADS // 2)], axis=1)
    values = other_ref[:, 2 * rows : 3 * rows, :].reshape(keys_total, HEAD_DIM)
    values = jnp.concatenate([values, jnp.ones_like(values)], axis=1)
    lane = lax.broadcasted_iota(jnp.int32, (HEAD_DIM, HEAD_DIM), 1)
    all_top = jnp.zeros((HEAD_DIM, HEAD_DIM), jnp.float32)
    all_total = jnp.ones((HEAD_DIM, HEAD_DIM), jnp.float32)
    for index in range(blocks):
        scores = next_scores
        if index + 1 < blocks:
            next_scores = score(index + 1)
        query_col = jnp.concatenate(
            [query_pos[:, index * tiles + i : index * tiles + i + 1] for i in range(tiles)], axis=0
        )
        scores = jnp.where(key_row <= query_col, scores, MASKED)
        top = jnp.broadcast_to(jnp.max(scores, axis=1, keepdims=True), (block, HEAD_DIM))
        here = slice(index * block, (index + 1) * block)
        if not first:
            old_top = top_in[here, :]
            top = jnp.maximum(top, old_top)
            factor = jnp.exp2((old_top - top) * SCALE2)
        weights = jnp.exp2((scores - top[:, 0:1]) * SCALE2).astype(jnp.bfloat16)
        summed = jnp.dot(weights, values, preferred_element_type=jnp.float32)
        acc, total = summed[:, :HEAD_DIM], summed[:, HEAD_DIM:]
        if not first:
            acc = acc + acc_in[here, :] * factor
            total = total + total_in[here, :] * factor
        if last:
            result = (acc * (1.0 / total)).astype(jnp.bfloat16)
            outs[0][index * GROUP : (index + 1) * GROUP, 0:rows, :] = result.reshape(
                GROUP, rows, HEAD_DIM
            )
            for i in range(tiles):
                tile = slice(i * HEAD_DIM, (i + 1) * HEAD_DIM)
                all_top = jnp.where(lane == index * tiles + i, top[tile], all_top)
                all_total = jnp.where(lane == index * tiles + i, total[tile], all_total)
        else:
            outs[0][here, :] = acc
            outs[1][here, :] = total
            outs[2][here, :] = top
    if last:
        pairs = HEADS // 2
        log_total = jnp.transpose(all_top)[0:pairs] * SCALE
        log_total = log_total + jnp.log(jnp.transpose(all_total)[0:pairs])
        high = log_total.astype(jnp.bfloat16).astype(jnp.float32)
        middle = (log_total - high).astype(jnp.bfloat16).astype(jnp.float32)
        low = log_total - high - middle
        row = lax.broadcasted_iota(jnp.int32, (EXTRA, HEAD_DIM), 0)
        for pair in range(pairs):
            terms = [
                jnp.broadcast_to(term[pair : pair + 1, :], (EXTRA, HEAD_DIM))
                for term in (high, middle, low)
            ]
            extra = jnp.where(row == 0, terms[0], jnp.where(row == 1, terms[1], terms[2]))
            extra = extra.astype(jnp.bfloat16)
            for i in range(2):
                outs[0][2 * pair + i, rows : rows + EXTRA, :] = extra


def unpack_kernel(in_ref, out_ref, log_ref):
    rows = out_ref.shape[0]
    for head in range(HEADS):
        out_ref[:, head * HEAD_DIM : (head + 1) * HEAD_DIM] = in_ref[head, 0:rows, :]
    extra = in_ref[:, rows : rows + EXTRA, :].astype(jnp.float32)
    log_total = extra[:, 0, :] + extra[:, 1, :] + extra[:, 2, :]
    half = lax.axis_index("head") % 2
    log_ref[...] = jnp.where(half == 0, log_total[:, 0:rows], log_total[:, rows : 2 * rows])


def params():
    return pltpu.CompilerParams(vmem_limit_bytes=VMEM_LIMIT)


def local(queries, keys, values, span_order):
    rows = queries.shape[0]
    parts = lax.axis_size("part")
    in_hbm = [
        pltpu.with_memory_space_constraint(array, pltpu.HBM)
        for array in (span_order, queries, keys, values)
    ]
    packed = pl.pallas_call(
        pack_kernel,
        out_shape=jax.ShapeDtypeStruct((HEADS, 3 * rows + EXTRA, HEAD_DIM), jnp.bfloat16),
        in_specs=[HBM] * 4,
        out_specs=VMEM,
        scratch_shapes=[
            pltpu.SMEM(span_order.shape, jnp.int32),
            pltpu.VMEM((3,) + queries.shape, jnp.bfloat16),
            pltpu.SemaphoreType.DMA((4,)),
        ],
        compiler_params=params(),
    )(*in_hbm)
    mine = lax.all_to_all(packed, "head", 0, 0, tiled=True)
    total_rows = HEADS * rows
    ring = [(i, (i + 1) % parts) for i in range(parts)]
    state = ()
    other = mine
    for part in range(parts):
        first, last = part == 0, part == parts - 1
        if last:
            shapes = (jax.ShapeDtypeStruct((HEADS, rows + EXTRA, HEAD_DIM), jnp.bfloat16),)
            following = None
        else:
            shapes = (jax.ShapeDtypeStruct((total_rows, HEAD_DIM), jnp.float32),) * 3
            following = lax.ppermute(other, "part", ring)
        state = pl.pallas_call(
            functools.partial(attend_kernel, first, last),
            out_shape=shapes,
            in_specs=[VMEM] * (2 + len(state)),
            out_specs=(VMEM,) * len(shapes),
            compiler_params=params(),
            cost_estimate=pl.CostEstimate(
                flops=4 * total_rows * total_rows * HEAD_DIM,
                bytes_accessed=1 << 20,
                transcendentals=total_rows * total_rows,
            ),
        )(mine, other, *state)
        other = following
    back = lax.all_to_all(state[0], "head", 0, 0, tiled=True)
    return pl.pallas_call(
        unpack_kernel,
        out_shape=(
            jax.ShapeDtypeStruct((rows, HEADS * HEAD_DIM), jnp.bfloat16),
            jax.ShapeDtypeStruct((HEADS, rows), jnp.float32),
        ),
        in_specs=[VMEM],
        out_specs=(VMEM, VMEM),
        compiler_params=params(),
    )(back)


def solution(mesh):
    rows = P(("head", "part"), None)
    return jax.shard_map(
        local,
        mesh=Mesh(mesh.devices.reshape(HEADS, -1), ("head", "part")),
        in_specs=(rows, rows, rows, P(("head", "part"))),
        out_specs=(rows, P(None, ("head", "part"))),
        check_vma=False,
    )
```

```python
import functools
import math

import jax
import jax.numpy as jnp
from jax import lax
from jax.experimental import pallas as pl
from jax.experimental.pallas import tpu as pltpu
from jax.sharding import Mesh
from jax.sharding import PartitionSpec as P

HEADS = 16
HEAD_DIM = 128
SPAN = 32
DIGIT = 64
SPANS = 2
SOURCES = HEADS * SPANS
QUARTERS = HEAD_DIM // SPAN
EXTRA = 2
GROUP = 8
MASKED = -1e30
SCALE = 1.0 / math.sqrt(HEAD_DIM)
SCALE2 = SCALE * math.log2(math.e)
VMEM_LIMIT = 48 * 1024 * 1024

VMEM = pl.BlockSpec(memory_space=pltpu.VMEM)
HBM = pl.BlockSpec(memory_space=pltpu.HBM)


def flat(ref):
    count, half, two, lanes = ref.shape
    return ref.reshape(count, half * two, lanes)


def messages(rows):
    return jax.ShapeDtypeStruct((SOURCES, (rows + EXTRA) // 2, 2, HEAD_DIM), jnp.bfloat16)


def quarter(exchange):
    return lax.axis_index(exchange) % QUARTERS


def pack_kernel(exchange, span_hbm, q_hbm, k_hbm, v_hbm, out_ref, ranks, buffers, sems):
    span_copy = pltpu.make_async_copy(span_hbm, ranks, sems.at[3])
    span_copy.start()
    copies = [
        pltpu.make_async_copy(source, buffers.at[i], sems.at[i])
        for i, source in enumerate((q_hbm, k_hbm, v_hbm))
    ]
    for copy in copies:
        copy.start()
    out = flat(out_ref)
    span_copy.wait()
    lane = lax.broadcasted_iota(jnp.int32, (EXTRA, HEAD_DIM), 1)
    row = lax.broadcasted_iota(jnp.int32, (EXTRA, HEAD_DIM), 0)
    for span in range(SPANS):
        digit = jnp.where(row == 0, ranks[span] // DIGIT, ranks[span] % DIGIT)
        extra = jnp.where(lane // SPAN == quarter(exchange), digit, 0)
        extra = extra.astype(jnp.float32).astype(jnp.bfloat16)
        for head in range(HEADS):
            out[SPANS * head + span, 3 * SPAN : 3 * SPAN + EXTRA, :] = extra
    for i, copy in enumerate(copies):
        copy.wait()
        for head in range(HEADS):
            for span in range(SPANS):
                out[SPANS * head + span, i * SPAN : (i + 1) * SPAN, :] = buffers[
                    i, span * SPAN : (span + 1) * SPAN, head * HEAD_DIM : (head + 1) * HEAD_DIM
                ]


def positions(ref):
    extra = flat(ref)[:, 3 * SPAN : 3 * SPAN + EXTRA, :].astype(jnp.float32)
    rank = extra[:, 0, :] * DIGIT + extra[:, 1, :]
    rank = jnp.sum(rank.reshape(SOURCES // QUARTERS, QUARTERS, HEAD_DIM), axis=1)
    lane = lax.broadcasted_iota(jnp.int32, rank.shape, 1)
    return rank * SPAN + (lane % SPAN).astype(jnp.float32)


def attend_kernel(first, last, mine_ref, other_ref, *refs):
    if first:
        outs = refs
    else:
        acc_in, total_in, top_in, *outs = refs
    mine, other = flat(mine_ref), flat(other_ref)
    block = GROUP * SPAN
    blocks = SOURCES // GROUP
    tiles = block // HEAD_DIM
    groups = SOURCES // QUARTERS
    keys = other[:, SPAN : 2 * SPAN, :].reshape(SOURCES * SPAN, HEAD_DIM)

    def score(index):
        queries = mine[index * GROUP : (index + 1) * GROUP, 0:SPAN, :]
        return lax.dot_general(
            queries.reshape(block, HEAD_DIM),
            keys,
            (((1,), (1,)), ((), ())),
            preferred_element_type=jnp.float32,
        )

    next_scores = score(0)
    query_pos = jnp.concatenate([positions(mine_ref)] * (HEAD_DIM // groups), axis=0)
    query_pos = jnp.transpose(query_pos)
    key_pos = positions(other_ref)
    key_row = jnp.concatenate([key_pos[i : i + 1, :] for i in range(groups)], axis=1)
    values = other[:, 2 * SPAN : 3 * SPAN, :].reshape(SOURCES * SPAN, HEAD_DIM)
    values = jnp.concatenate([values, jnp.ones_like(values)], axis=1)
    lane = lax.broadcasted_iota(jnp.int32, (HEAD_DIM, HEAD_DIM), 1)
    all_top = jnp.zeros((HEAD_DIM, HEAD_DIM), jnp.float32)
    all_total = jnp.ones((HEAD_DIM, HEAD_DIM), jnp.float32)
    for index in range(blocks):
        scores = next_scores
        if index + 1 < blocks:
            next_scores = score(index + 1)
        query_col = jnp.concatenate(
            [query_pos[:, index * tiles + i : index * tiles + i + 1] for i in range(tiles)], axis=0
        )
        scores = jnp.where(key_row <= query_col, scores, MASKED)
        top = jnp.broadcast_to(jnp.max(scores, axis=1, keepdims=True), (block, HEAD_DIM))
        here = slice(index * block, (index + 1) * block)
        if not first:
            old_top = top_in[here, :]
            top = jnp.maximum(top, old_top)
            factor = jnp.exp2((old_top - top) * SCALE2)
        weights = jnp.exp2((scores - top[:, 0:1]) * SCALE2).astype(jnp.bfloat16)
        summed = jnp.dot(weights, values, preferred_element_type=jnp.float32)
        acc, total = summed[:, :HEAD_DIM], summed[:, HEAD_DIM:]
        if not first:
            acc = acc + acc_in[here, :] * factor
            total = total + total_in[here, :] * factor
        if last:
            result = (acc * (1.0 / total)).astype(jnp.bfloat16)
            flat(outs[0])[index * GROUP : (index + 1) * GROUP, 0:SPAN, :] = result.reshape(
                GROUP, SPAN, HEAD_DIM
            )
            for i in range(tiles):
                tile = slice(i * HEAD_DIM, (i + 1) * HEAD_DIM)
                all_top = jnp.where(lane == index * tiles + i, top[tile], all_top)
                all_total = jnp.where(lane == index * tiles + i, total[tile], all_total)
        else:
            outs[0][here, :] = acc
            outs[1][here, :] = total
            outs[2][here, :] = top
    if last:
        log_total = jnp.transpose(all_top)[0:groups] * SCALE
        log_total = log_total + jnp.log(jnp.transpose(all_total)[0:groups])
        high = log_total.astype(jnp.bfloat16).astype(jnp.float32)
        low = log_total - high
        row = lax.broadcasted_iota(jnp.int32, (EXTRA, HEAD_DIM), 0)
        for i in range(groups):
            extra = jnp.where(row == 0, high[i : i + 1, :], low[i : i + 1, :])
            extra = extra.astype(jnp.bfloat16)
            for j in range(QUARTERS):
                flat(outs[0])[QUARTERS * i + j, SPAN : SPAN + EXTRA, :] = extra


def unpack_kernel(exchange, in_ref, out_ref, log_ref):
    back = flat(in_ref)
    for head in range(HEADS):
        for span in range(SPANS):
            out_ref[
                span * SPAN : (span + 1) * SPAN, head * HEAD_DIM : (head + 1) * HEAD_DIM
            ] = back[SPANS * head + span, 0:SPAN, :]
    extra = back[:, SPAN : SPAN + EXTRA, :].astype(jnp.float32)
    log_total = (extra[:, 0, :] + extra[:, 1, :]).reshape(HEADS, SPANS, HEAD_DIM)
    mine = log_total[:, :, 0:SPAN]
    for i in range(1, QUARTERS):
        mine = jnp.where(quarter(exchange) == i, log_total[:, :, i * SPAN : (i + 1) * SPAN], mine)
    for span in range(SPANS):
        log_ref[:, span * SPAN : (span + 1) * SPAN] = mine[:, span, :]


def params():
    return pltpu.CompilerParams(vmem_limit_bytes=VMEM_LIMIT)


def local(everywhere, exchange, queries, keys, values, span_order):
    rows = queries.shape[0]
    devices = lax.axis_size(everywhere)
    parts = devices // HEADS
    in_hbm = [
        pltpu.with_memory_space_constraint(array, pltpu.HBM)
        for array in (span_order, queries, keys, values)
    ]
    packed = pl.pallas_call(
        functools.partial(pack_kernel, exchange),
        out_shape=messages(3 * SPAN),
        in_specs=[HBM] * 4,
        out_specs=VMEM,
        scratch_shapes=[
            pltpu.SMEM(span_order.shape, jnp.int32),
            pltpu.VMEM((3,) + queries.shape, jnp.bfloat16),
            pltpu.SemaphoreType.DMA((4,)),
        ],
        compiler_params=params(),
    )(*in_hbm)
    mine = lax.all_to_all(packed, exchange, 0, 0, tiled=True)
    total_rows = SOURCES * SPAN
    ring = [(i, i // parts * parts + (i + 1) % parts) for i in range(devices)]
    state = ()
    other = mine
    for part in range(parts):
        first, last = part == 0, part == parts - 1
        if last:
            shapes = (messages(SPAN),)
            following = None
        else:
            shapes = (jax.ShapeDtypeStruct((total_rows, HEAD_DIM), jnp.float32),) * 3
            following = lax.ppermute(other, everywhere, ring)
        state = pl.pallas_call(
            functools.partial(attend_kernel, first, last),
            out_shape=shapes,
            in_specs=[VMEM] * (2 + len(state)),
            out_specs=(VMEM,) * len(shapes),
            compiler_params=params(),
            cost_estimate=pl.CostEstimate(
                flops=4 * total_rows * total_rows * HEAD_DIM,
                bytes_accessed=1 << 20,
                transcendentals=total_rows * total_rows,
            ),
        )(mine, other, *state)
        other = following
    back = lax.all_to_all(state[0], exchange, 0, 0, tiled=True)
    return pl.pallas_call(
        functools.partial(unpack_kernel, exchange),
        out_shape=(
            jax.ShapeDtypeStruct((rows, HEADS * HEAD_DIM), jnp.bfloat16),
            jax.ShapeDtypeStruct((HEADS, rows), jnp.float32),
        ),
        in_specs=[VMEM],
        out_specs=(VMEM, VMEM),
        compiler_params=params(),
    )(back)


def solution(mesh):
    devices = mesh.devices.reshape(HEADS, -1, SPANS)
    if devices.shape[1] == 1:
        devices, everywhere, exchange = devices.reshape(-1), ("source",), ("source",)
    else:
        everywhere, exchange = ("head", "ring", "core"), ("head", "core")
    rows = P(everywhere, None)
    return jax.shard_map(
        functools.partial(local, everywhere, exchange),
        mesh=Mesh(devices, everywhere),
        in_specs=(rows, rows, rows, P(everywhere)),
        out_specs=(rows, P(None, everywhere)),
        check_vma=False,
    )
```

```python
import functools
import math

import jax
import jax.numpy as jnp
from jax import lax
from jax.experimental import pallas as pl
from jax.experimental.pallas import tpu as pltpu
from jax.sharding import Mesh
from jax.sharding import PartitionSpec as P

HEADS = 16
HEAD_DIM = 128
SPAN = 32
DIGIT = 64
SPANS = 2
SOURCES = HEADS * SPANS
QUARTERS = HEAD_DIM // SPAN
EXTRA = 2
THERE = 3 * SPAN + EXTRA
BACK = SPAN + EXTRA
GROUP = 8
MASKED = -1e30
SCALE = 1.0 / math.sqrt(HEAD_DIM)
SCALE2 = SCALE * math.log2(math.e)
VMEM_LIMIT = 48 * 1024 * 1024

VMEM = pl.BlockSpec(memory_space=pltpu.VMEM)
HBM = pl.BlockSpec(memory_space=pltpu.HBM)


def rows_of(message, size, first, count):
    return slice(message * size + first, message * size + first + count)


def messages(size):
    return jax.ShapeDtypeStruct((SOURCES * size, HEAD_DIM), jnp.bfloat16)


def exchanged(array, exchange):
    paired = array.reshape(SOURCES, -1, 2, HEAD_DIM)
    return lax.all_to_all(paired, exchange, 0, 0, tiled=True).reshape(array.shape)


def quarter(exchange):
    return lax.axis_index(exchange) % QUARTERS


def pack_kernel(exchange, span_hbm, q_hbm, k_hbm, v_hbm, out_ref, ranks, buffers, sems):
    span_copy = pltpu.make_async_copy(span_hbm, ranks, sems.at[3])
    span_copy.start()
    copies = [
        pltpu.make_async_copy(source, buffers.at[i], sems.at[i])
        for i, source in enumerate((q_hbm, k_hbm, v_hbm))
    ]
    for copy in copies:
        copy.start()
    span_copy.wait()
    lane = lax.broadcasted_iota(jnp.int32, (EXTRA, HEAD_DIM), 1)
    row = lax.broadcasted_iota(jnp.int32, (EXTRA, HEAD_DIM), 0)
    for span in range(SPANS):
        digit = jnp.where(row == 0, ranks[span] // DIGIT, ranks[span] % DIGIT)
        extra = jnp.where(lane // SPAN == quarter(exchange), digit, 0)
        extra = extra.astype(jnp.float32).astype(jnp.bfloat16)
        for head in range(HEADS):
            out_ref[rows_of(SPANS * head + span, THERE, 3 * SPAN, EXTRA), :] = extra
    for i, copy in enumerate(copies):
        copy.wait()
        for head in range(HEADS):
            for span in range(SPANS):
                out_ref[rows_of(SPANS * head + span, THERE, i * SPAN, SPAN), :] = buffers[
                    i, span * SPAN : (span + 1) * SPAN, head * HEAD_DIM : (head + 1) * HEAD_DIM
                ]


def positions(ref):
    ranks = []
    for i in range(0, SOURCES, QUARTERS):
        extras = [ref[rows_of(i + j, THERE, 3 * SPAN, EXTRA), :] for j in range(QUARTERS)]
        digits = sum(extra.astype(jnp.float32) for extra in extras)
        ranks.append(digits[0:1] * DIGIT + digits[1:2])
    rank = jnp.concatenate(ranks, axis=0)
    lane = lax.broadcasted_iota(jnp.int32, rank.shape, 1)
    return rank * SPAN + (lane % SPAN).astype(jnp.float32)


def spans(ref, sources, which):
    return jnp.concatenate(
        [ref[rows_of(source, THERE, which * SPAN, SPAN), :] for source in sources], axis=0
    )


def attend_kernel(first, last, mine_ref, other_ref, *refs):
    if first:
        outs = refs
    else:
        acc_in, total_in, top_in, *outs = refs
    block = GROUP * SPAN
    blocks = SOURCES // GROUP
    tiles = block // HEAD_DIM
    groups = SOURCES // QUARTERS
    keys = spans(other_ref, range(SOURCES), 1)

    def score(index):
        return lax.dot_general(
            spans(mine_ref, range(index * GROUP, (index + 1) * GROUP), 0),
            keys,
            (((1,), (1,)), ((), ())),
            preferred_element_type=jnp.float32,
        )

    next_scores = score(0)
    query_pos = jnp.concatenate([positions(mine_ref)] * (HEAD_DIM // groups), axis=0)
    query_pos = jnp.transpose(query_pos)
    key_pos = positions(other_ref)
    key_row = jnp.concatenate([key_pos[i : i + 1, :] for i in range(groups)], axis=1)
    values = spans(other_ref, range(SOURCES), 2)
    values = jnp.concatenate([values, jnp.ones_like(values)], axis=1)
    lane = lax.broadcasted_iota(jnp.int32, (HEAD_DIM, HEAD_DIM), 1)
    all_top = jnp.zeros((HEAD_DIM, HEAD_DIM), jnp.float32)
    all_total = jnp.ones((HEAD_DIM, HEAD_DIM), jnp.float32)
    for index in range(blocks):
        scores = next_scores
        if index + 1 < blocks:
            next_scores = score(index + 1)
        query_col = jnp.concatenate(
            [query_pos[:, index * tiles + i : index * tiles + i + 1] for i in range(tiles)], axis=0
        )
        scores = jnp.where(key_row <= query_col, scores, MASKED)
        top = jnp.broadcast_to(jnp.max(scores, axis=1, keepdims=True), (block, HEAD_DIM))
        here = slice(index * block, (index + 1) * block)
        if not first:
            old_top = top_in[here, :]
            top = jnp.maximum(top, old_top)
            factor = jnp.exp2((old_top - top) * SCALE2)
        weights = jnp.exp2((scores - top[:, 0:1]) * SCALE2).astype(jnp.bfloat16)
        summed = jnp.dot(weights, values, preferred_element_type=jnp.float32)
        acc, total = summed[:, :HEAD_DIM], summed[:, HEAD_DIM:]
        if not first:
            acc = acc + acc_in[here, :] * factor
            total = total + total_in[here, :] * factor
        if last:
            result = (acc * (1.0 / total)).astype(jnp.bfloat16)
            for i in range(GROUP):
                place = rows_of(index * GROUP + i, BACK, 0, SPAN)
                outs[0][place, :] = result[i * SPAN : (i + 1) * SPAN]
            for i in range(tiles):
                tile = slice(i * HEAD_DIM, (i + 1) * HEAD_DIM)
                all_top = jnp.where(lane == index * tiles + i, top[tile], all_top)
                all_total = jnp.where(lane == index * tiles + i, total[tile], all_total)
        else:
            outs[0][here, :] = acc
            outs[1][here, :] = total
            outs[2][here, :] = top
    if last:
        log_total = jnp.transpose(all_top)[0:groups] * SCALE
        log_total = log_total + jnp.log(jnp.transpose(all_total)[0:groups])
        high = log_total.astype(jnp.bfloat16).astype(jnp.float32)
        low = log_total - high
        row = lax.broadcasted_iota(jnp.int32, (EXTRA, HEAD_DIM), 0)
        for i in range(groups):
            extra = jnp.where(row == 0, high[i : i + 1, :], low[i : i + 1, :])
            extra = extra.astype(jnp.bfloat16)
            for j in range(QUARTERS):
                outs[0][rows_of(QUARTERS * i + j, BACK, SPAN, EXTRA), :] = extra


def unpack_kernel(exchange, in_ref, out_ref, log_ref):
    mine = []
    for span in range(SPANS):
        extras = []
        for head in range(HEADS):
            source = SPANS * head + span
            out_ref[
                span * SPAN : (span + 1) * SPAN, head * HEAD_DIM : (head + 1) * HEAD_DIM
            ] = in_ref[rows_of(source, BACK, 0, SPAN), :]
            terms = in_ref[rows_of(source, BACK, SPAN, EXTRA), :].astype(jnp.float32)
            extras.append(jnp.sum(terms, axis=0, keepdims=True))
        log_total = jnp.concatenate(extras, axis=0)
        here = log_total[:, 0:SPAN]
        for i in range(1, QUARTERS):
            here = jnp.where(quarter(exchange) == i, log_total[:, i * SPAN : (i + 1) * SPAN], here)
        mine.append(here)
    log_ref[...] = jnp.concatenate(mine, axis=1)


def params():
    return pltpu.CompilerParams(vmem_limit_bytes=VMEM_LIMIT)


def local(everywhere, exchange, queries, keys, values, span_order):
    rows = queries.shape[0]
    devices = lax.axis_size(everywhere)
    parts = devices // HEADS
    in_hbm = [
        pltpu.with_memory_space_constraint(array, pltpu.HBM)
        for array in (span_order, queries, keys, values)
    ]
    packed = pl.pallas_call(
        functools.partial(pack_kernel, exchange),
        out_shape=messages(THERE),
        in_specs=[HBM] * 4,
        out_specs=VMEM,
        scratch_shapes=[
            pltpu.SMEM(span_order.shape, jnp.int32),
            pltpu.VMEM((3,) + queries.shape, jnp.bfloat16),
            pltpu.SemaphoreType.DMA((4,)),
        ],
        compiler_params=params(),
    )(*in_hbm)
    mine = exchanged(packed, exchange)
    total_rows = SOURCES * SPAN
    ring = [(i, i // parts * parts + (i + 1) % parts) for i in range(devices)]
    state = ()
    other = mine
    for part in range(parts):
        first, last = part == 0, part == parts - 1
        if last:
            shapes = (messages(BACK),)
            following = None
        else:
            shapes = (jax.ShapeDtypeStruct((total_rows, HEAD_DIM), jnp.float32),) * 3
            following = lax.ppermute(other, everywhere, ring)
        state = pl.pallas_call(
            functools.partial(attend_kernel, first, last),
            out_shape=shapes,
            in_specs=[VMEM] * (2 + len(state)),
            out_specs=(VMEM,) * len(shapes),
            compiler_params=params(),
            cost_estimate=pl.CostEstimate(
                flops=4 * total_rows * total_rows * HEAD_DIM,
                bytes_accessed=1 << 20,
                transcendentals=total_rows * total_rows,
            ),
        )(mine, other, *state)
        other = following
    back = exchanged(state[0], exchange)
    return pl.pallas_call(
        functools.partial(unpack_kernel, exchange),
        out_shape=(
            jax.ShapeDtypeStruct((rows, HEADS * HEAD_DIM), jnp.bfloat16),
            jax.ShapeDtypeStruct((HEADS, rows), jnp.float32),
        ),
        in_specs=[VMEM],
        out_specs=(VMEM, VMEM),
        compiler_params=params(),
    )(back)


def solution(mesh):
    devices = mesh.devices.reshape(HEADS, -1, SPANS)
    if devices.shape[1] == 1:
        devices, everywhere, exchange = devices.reshape(-1), ("source",), ("source",)
    else:
        everywhere, exchange = ("head", "ring", "core"), ("head", "core")
    rows = P(everywhere, None)
    return jax.shard_map(
        functools.partial(local, everywhere, exchange),
        mesh=Mesh(devices, everywhere),
        in_specs=(rows, rows, rows, P(everywhere)),
        out_specs=(rows, P(None, everywhere)),
        check_vma=False,
    )
```

```python
import functools
import math

import jax
import jax.numpy as jnp
from jax import lax
from jax.experimental import pallas as pl
from jax.experimental.pallas import tpu as pltpu
from jax.sharding import Mesh
from jax.sharding import PartitionSpec as P

HEADS = 16
HEAD_DIM = 128
SPAN = 32
DIGIT = 64
SPANS = 2
SOURCES = HEADS * SPANS
QUARTERS = HEAD_DIM // SPAN
EXTRA = 2
THERE = 3 * SPAN + EXTRA
BACK = SPAN + EXTRA
GROUP = 8
STEP = 8
MASKED = -1e30
SCALE = 1.0 / math.sqrt(HEAD_DIM)
SCALE2 = SCALE * math.log2(math.e)
VMEM_LIMIT = 48 * 1024 * 1024

VMEM = pl.BlockSpec(memory_space=pltpu.VMEM)
HBM = pl.BlockSpec(memory_space=pltpu.HBM)


def rows_of(message, size, first, count):
    return slice(message * size + first, message * size + first + count)


def messages(size):
    return jax.ShapeDtypeStruct((SOURCES * size, HEAD_DIM), jnp.bfloat16)


def exchanged(array, exchange):
    paired = array.reshape(SOURCES, -1, 2, HEAD_DIM)
    return lax.all_to_all(paired, exchange, 0, 0, tiled=True).reshape(array.shape)


def quarter(exchange):
    return lax.axis_index(exchange) % QUARTERS


def pack_kernel(exchange, span_hbm, q_hbm, k_hbm, v_hbm, out_ref, ranks, buffers, sems):
    span_copy = pltpu.make_async_copy(span_hbm, ranks, sems.at[3])
    span_copy.start()
    copies = [
        pltpu.make_async_copy(source, buffers.at[i], sems.at[i])
        for i, source in enumerate((q_hbm, k_hbm, v_hbm))
    ]
    for copy in copies:
        copy.start()
    span_copy.wait()
    lane = lax.broadcasted_iota(jnp.int32, (EXTRA, HEAD_DIM), 1)
    row = lax.broadcasted_iota(jnp.int32, (EXTRA, HEAD_DIM), 0)
    for span in range(SPANS):
        digit = jnp.where(row == 0, ranks[span] // DIGIT, ranks[span] % DIGIT)
        extra = jnp.where(lane // SPAN == quarter(exchange), digit, 0)
        extra = extra.astype(jnp.float32).astype(jnp.bfloat16)
        for head in range(HEADS):
            out_ref[rows_of(SPANS * head + span, THERE, 3 * SPAN, EXTRA), :] = extra
    for i, copy in enumerate(copies):
        copy.wait()
        for head in range(HEADS):
            for span in range(SPANS):
                out_ref[rows_of(SPANS * head + span, THERE, i * SPAN, SPAN), :] = buffers[
                    i, span * SPAN : (span + 1) * SPAN, head * HEAD_DIM : (head + 1) * HEAD_DIM
                ]


def positions(ref):
    ranks = []
    for i in range(0, SOURCES, QUARTERS):
        extras = [ref[rows_of(i + j, THERE, 3 * SPAN, EXTRA), :] for j in range(QUARTERS)]
        digits = sum(extra.astype(jnp.float32) for extra in extras)
        ranks.append(digits[0:1] * DIGIT + digits[1:2])
    rank = jnp.concatenate(ranks, axis=0)
    lane = lax.broadcasted_iota(jnp.int32, rank.shape, 1)
    return rank * SPAN + (lane % SPAN).astype(jnp.float32)


def spans(ref, sources, which):
    return jnp.concatenate(
        [ref[rows_of(source, THERE, which * SPAN, SPAN), :] for source in sources], axis=0
    )


def attend_kernel(exchange, first, last, mine_ref, other_ref, *refs):
    if first:
        outs = refs
    else:
        acc_in, total_in, top_in, *outs = refs
    block = GROUP * SPAN
    blocks = SOURCES // GROUP
    tiles = SOURCES // QUARTERS
    keys = spans(other_ref, range(SOURCES), 1)
    key_pos = positions(other_ref)
    query_pos = key_pos if first else positions(mine_ref)
    key_tiles = [jnp.broadcast_to(key_pos[t : t + 1, :], (STEP, HEAD_DIM)) for t in range(tiles)]
    lane = lax.broadcasted_iota(jnp.int32, (STEP, HEAD_DIM), 1)
    row = lax.broadcasted_iota(jnp.int32, (STEP, HEAD_DIM), 0)

    def score(index):
        sources = range(index * GROUP, (index + 1) * GROUP)
        scores = lax.dot_general(
            spans(mine_ref, sources, 0),
            keys,
            (((1,), (1,)), ((), ())),
            preferred_element_type=jnp.float32,
        )
        masked = [[] for _ in range(tiles)]
        for i, source in enumerate(sources):
            tile, lead = source // QUARTERS, source % QUARTERS * SPAN
            start = query_pos[tile : tile + 1, lead : lead + 1]
            before = [key_tiles[t] < start for t in range(tiles)]
            for j in range(0, SPAN, STEP):
                here = i * SPAN + j
                for t in range(tiles):
                    visible = before[t]
                    if first and t == tile:
                        visible = visible | ((lane >= lead) & (lane - lead <= row + j))
                    piece = scores[here : here + STEP, t * HEAD_DIM : (t + 1) * HEAD_DIM]
                    masked[t].append(jnp.where(visible, piece, MASKED))
        masked = [jnp.concatenate(pieces, axis=0) for pieces in masked]
        return masked, jnp.max(functools.reduce(jnp.maximum, masked), axis=1, keepdims=True)

    following = score(0)
    values = spans(other_ref, range(SOURCES), 2)
    values = jnp.concatenate([values, jnp.ones_like(values)], axis=1)
    square_lane = lax.broadcasted_iota(jnp.int32, (HEAD_DIM, HEAD_DIM), 1)
    all_top = jnp.zeros((HEAD_DIM, HEAD_DIM), jnp.float32)
    all_total = jnp.ones((HEAD_DIM, HEAD_DIM), jnp.float32)
    for index in range(blocks):
        masked, top = following
        if index + 1 < blocks:
            following = score(index + 1)
        here = slice(index * block, (index + 1) * block)
        top = jnp.broadcast_to(top, (block, HEAD_DIM))
        if not first:
            old_top = top_in[here, :]
            top = jnp.maximum(top, old_top)
            factor = jnp.exp2((old_top - top) * SCALE2)
        weights = [jnp.exp2((piece - top) * SCALE2).astype(jnp.bfloat16) for piece in masked]
        summed = jnp.dot(
            jnp.concatenate(weights, axis=1), values, preferred_element_type=jnp.float32
        )
        acc, total = summed[:, :HEAD_DIM], summed[:, HEAD_DIM:]
        if not first:
            acc = acc + acc_in[here, :] * factor
            total = total + total_in[here, :] * factor
        if last:
            result = (acc * (1.0 / total)).astype(jnp.bfloat16)
            for i in range(GROUP):
                place = rows_of(index * GROUP + i, BACK, 0, SPAN)
                outs[0][place, :] = result[i * SPAN : (i + 1) * SPAN]
            for i in range(GROUP // QUARTERS):
                rows = slice(i * HEAD_DIM, (i + 1) * HEAD_DIM)
                chosen = square_lane == index * (GROUP // QUARTERS) + i
                all_top = jnp.where(chosen, top[rows], all_top)
                all_total = jnp.where(chosen, total[rows], all_total)
        else:
            outs[0][here, :] = acc
            outs[1][here, :] = total
            outs[2][here, :] = top
    if last:
        log_total = jnp.transpose(all_top)[0:tiles] * SCALE
        log_total = log_total + jnp.log(jnp.transpose(all_total)[0:tiles])
        high = log_total.astype(jnp.bfloat16).astype(jnp.float32)
        low = log_total - high
        span = lax.axis_index(exchange) % SPANS
        kept = lane // SPAN == span
        for j in range(QUARTERS):
            shift = ((span - j) % QUARTERS) * SPAN
            terms = [jnp.where(kept, pltpu.roll(term, shift, 1), 0.0) for term in (high, low)]
            for i in range(tiles):
                extra = jnp.concatenate([term[i : i + 1, :] for term in terms], axis=0)
                outs[0][rows_of(QUARTERS * i + j, BACK, SPAN, EXTRA), :] = extra.astype(
                    jnp.bfloat16
                )


def unpack_kernel(in_ref, out_ref, log_ref):
    log_totals = []
    for head in range(HEADS):
        terms = 0.0
        for span in range(SPANS):
            source = SPANS * head + span
            out_ref[
                span * SPAN : (span + 1) * SPAN, head * HEAD_DIM : (head + 1) * HEAD_DIM
            ] = in_ref[rows_of(source, BACK, 0, SPAN), :]
            terms += in_ref[rows_of(source, BACK, SPAN, EXTRA), :].astype(jnp.float32)
        log_totals.append(terms[0:1, :] + terms[1:2, :])
    log_ref[...] = jnp.concatenate(log_totals, axis=0)[:, 0 : SPANS * SPAN]


def params():
    return pltpu.CompilerParams(vmem_limit_bytes=VMEM_LIMIT)


def local(everywhere, exchange, queries, keys, values, span_order):
    rows = queries.shape[0]
    devices = lax.axis_size(everywhere)
    parts = devices // HEADS
    in_hbm = [
        pltpu.with_memory_space_constraint(array, pltpu.HBM)
        for array in (span_order, queries, keys, values)
    ]
    packed = pl.pallas_call(
        functools.partial(pack_kernel, exchange),
        out_shape=messages(THERE),
        in_specs=[HBM] * 4,
        out_specs=VMEM,
        scratch_shapes=[
            pltpu.SMEM(span_order.shape, jnp.int32),
            pltpu.VMEM((3,) + queries.shape, jnp.bfloat16),
            pltpu.SemaphoreType.DMA((4,)),
        ],
        compiler_params=params(),
    )(*in_hbm)
    mine = exchanged(packed, exchange)
    total_rows = SOURCES * SPAN
    ring = [(i, i // parts * parts + (i + 1) % parts) for i in range(devices)]
    state = ()
    other = mine
    for part in range(parts):
        first, last = part == 0, part == parts - 1
        if last:
            shapes = (messages(BACK),)
            following = None
        else:
            shapes = (jax.ShapeDtypeStruct((total_rows, HEAD_DIM), jnp.float32),) * 3
            following = lax.ppermute(other, everywhere, ring)
        state = pl.pallas_call(
            functools.partial(attend_kernel, exchange, first, last),
            out_shape=shapes,
            in_specs=[VMEM] * (2 + len(state)),
            out_specs=(VMEM,) * len(shapes),
            compiler_params=params(),
            cost_estimate=pl.CostEstimate(
                flops=4 * total_rows * total_rows * HEAD_DIM,
                bytes_accessed=1 << 20,
                transcendentals=total_rows * total_rows,
            ),
        )(mine, other, *state)
        other = following
    back = exchanged(state[0], exchange)
    return pl.pallas_call(
        unpack_kernel,
        out_shape=(
            jax.ShapeDtypeStruct((rows, HEADS * HEAD_DIM), jnp.bfloat16),
            jax.ShapeDtypeStruct((HEADS, rows), jnp.float32),
        ),
        in_specs=[VMEM],
        out_specs=(VMEM, VMEM),
        compiler_params=params(),
    )(back)


def solution(mesh):
    devices = mesh.devices.reshape(HEADS, -1, SPANS)
    if devices.shape[1] == 1:
        devices, everywhere, exchange = devices.reshape(-1), ("source",), ("source",)
    else:
        everywhere, exchange = ("head", "ring", "core"), ("head", "core")
    rows = P(everywhere, None)
    return jax.shard_map(
        functools.partial(local, everywhere, exchange),
        mesh=Mesh(devices, everywhere),
        in_specs=(rows, rows, rows, P(everywhere)),
        out_specs=(rows, P(None, everywhere)),
        check_vma=False,
    )
```

```python
import functools
import math

import jax
import jax.numpy as jnp
from jax import lax
from jax.experimental import pallas as pl
from jax.experimental.pallas import tpu as pltpu
from jax.sharding import Mesh
from jax.sharding import PartitionSpec as P

HEADS = 16
HEAD_DIM = 128
SPAN = 32
DIGIT = 64
SPANS = 2
SOURCES = HEADS * SPANS
QUARTERS = HEAD_DIM // SPAN
EXTRA = 2
THERE = 3 * SPAN + EXTRA
BACK = SPAN + EXTRA
GROUP = 8
STEP = 8
THERE_ORDER = (
    0, 8, 16, 24, 2, 10, 18, 26, 1, 9, 17, 25, 3, 11, 19, 27, 4, 12, 20, 28, 6, 14, 22, 30, 5,
    13, 21, 29, 7, 15, 23, 31,
)
BACK_ORDER = THERE_ORDER
MASKED = -1e30
SCALE = 1.0 / math.sqrt(HEAD_DIM)
SCALE2 = SCALE * math.log2(math.e)
VMEM_LIMIT = 48 * 1024 * 1024

VMEM = pl.BlockSpec(memory_space=pltpu.VMEM)
HBM = pl.BlockSpec(memory_space=pltpu.HBM)


def rows_of(message, size, first, count):
    return slice(message * size + first, message * size + first + count)


def messages(size):
    return jax.ShapeDtypeStruct((SOURCES * size, HEAD_DIM), jnp.bfloat16)


def exchanged(array, order):
    parts = lax.axis_size("source") // HEADS
    groups = [
        [member // SPANS * parts + first + member % SPANS for member in order]
        for first in range(0, parts, SPANS)
    ]
    paired = array.reshape(SOURCES, -1, 2, HEAD_DIM)
    paired = lax.all_to_all(paired, "source", 0, 0, axis_index_groups=groups, tiled=True)
    return paired.reshape(array.shape)


def pack_kernel(span_hbm, q_hbm, k_hbm, v_hbm, out_ref, ranks, buffers, sems):
    span_copy = pltpu.make_async_copy(span_hbm, ranks, sems.at[3])
    span_copy.start()
    copies = [
        pltpu.make_async_copy(source, buffers.at[i], sems.at[i])
        for i, source in enumerate((q_hbm, k_hbm, v_hbm))
    ]
    for copy in copies:
        copy.start()
    span_copy.wait()
    row = lax.broadcasted_iota(jnp.int32, (EXTRA, HEAD_DIM), 0)
    digits = []
    for span in range(SPANS):
        digit = jnp.where(row == 0, ranks[span] // DIGIT, ranks[span] % DIGIT)
        digits.append(digit.astype(jnp.float32).astype(jnp.bfloat16))
    for place, member in enumerate(THERE_ORDER):
        out_ref[rows_of(place, THERE, 3 * SPAN, EXTRA), :] = digits[member % SPANS]
    for i, copy in enumerate(copies):
        copy.wait()
        for place, member in enumerate(THERE_ORDER):
            head, span = member // SPANS, member % SPANS
            out_ref[rows_of(place, THERE, i * SPAN, SPAN), :] = buffers[
                i, span * SPAN : (span + 1) * SPAN, head * HEAD_DIM : (head + 1) * HEAD_DIM
            ]


def positions(ref):
    lane = lax.broadcasted_iota(jnp.int32, (EXTRA, HEAD_DIM), 1)
    ranks = []
    for i in range(0, SOURCES, QUARTERS):
        digits = 0.0
        for j in range(QUARTERS):
            extra = ref[rows_of(i + j, THERE, 3 * SPAN, EXTRA), :].astype(jnp.float32)
            digits = jnp.where(lane // SPAN == j, extra, digits)
        ranks.append(digits[0:1] * DIGIT + digits[1:2])
    rank = jnp.concatenate(ranks, axis=0)
    lane = lax.broadcasted_iota(jnp.int32, rank.shape, 1)
    return rank * SPAN + (lane % SPAN).astype(jnp.float32)


def spans(ref, sources, which):
    return jnp.concatenate(
        [ref[rows_of(source, THERE, which * SPAN, SPAN), :] for source in sources], axis=0
    )


def home(source):
    return BACK_ORDER.index(THERE_ORDER[source])


def attend_kernel(first, last, mine_ref, other_ref, *refs):
    if first:
        outs = refs
    else:
        acc_in, total_in, top_in, *outs = refs
    block = GROUP * SPAN
    blocks = SOURCES // GROUP
    tiles = SOURCES // QUARTERS
    keys = spans(other_ref, range(SOURCES), 1)
    key_pos = positions(other_ref)
    query_pos = key_pos if first else positions(mine_ref)
    key_tiles = [jnp.broadcast_to(key_pos[t : t + 1, :], (STEP, HEAD_DIM)) for t in range(tiles)]
    lane = lax.broadcasted_iota(jnp.int32, (STEP, HEAD_DIM), 1)
    row = lax.broadcasted_iota(jnp.int32, (STEP, HEAD_DIM), 0)

    def score(index):
        sources = range(index * GROUP, (index + 1) * GROUP)
        scores = lax.dot_general(
            spans(mine_ref, sources, 0),
            keys,
            (((1,), (1,)), ((), ())),
            preferred_element_type=jnp.float32,
        )
        masked = [[] for _ in range(tiles)]
        for i, source in enumerate(sources):
            tile, lead = source // QUARTERS, source % QUARTERS * SPAN
            start = query_pos[tile : tile + 1, lead : lead + 1]
            before = [key_tiles[t] < start for t in range(tiles)]
            for j in range(0, SPAN, STEP):
                here = i * SPAN + j
                for t in range(tiles):
                    visible = before[t]
                    if first and t == tile:
                        visible = visible | ((lane >= lead) & (lane - lead <= row + j))
                    piece = scores[here : here + STEP, t * HEAD_DIM : (t + 1) * HEAD_DIM]
                    masked[t].append(jnp.where(visible, piece, MASKED))
        masked = [jnp.concatenate(pieces, axis=0) for pieces in masked]
        return masked, jnp.max(functools.reduce(jnp.maximum, masked), axis=1, keepdims=True)

    following = score(0)
    values = spans(other_ref, range(SOURCES), 2)
    values = jnp.concatenate([values, jnp.ones_like(values)], axis=1)
    square_lane = lax.broadcasted_iota(jnp.int32, (HEAD_DIM, HEAD_DIM), 1)
    all_top = jnp.zeros((HEAD_DIM, HEAD_DIM), jnp.float32)
    all_total = jnp.ones((HEAD_DIM, HEAD_DIM), jnp.float32)
    for index in range(blocks):
        masked, top = following
        if index + 1 < blocks:
            following = score(index + 1)
        here = slice(index * block, (index + 1) * block)
        top = jnp.broadcast_to(top, (block, HEAD_DIM))
        if not first:
            old_top = top_in[here, :]
            top = jnp.maximum(top, old_top)
            factor = jnp.exp2((old_top - top) * SCALE2)
        weights = [jnp.exp2((piece - top) * SCALE2).astype(jnp.bfloat16) for piece in masked]
        summed = jnp.dot(
            jnp.concatenate(weights, axis=1), values, preferred_element_type=jnp.float32
        )
        acc, total = summed[:, :HEAD_DIM], summed[:, HEAD_DIM:]
        if not first:
            acc = acc + acc_in[here, :] * factor
            total = total + total_in[here, :] * factor
        if last:
            result = (acc * (1.0 / total)).astype(jnp.bfloat16)
            for i in range(GROUP):
                outs[0][rows_of(home(index * GROUP + i), BACK, 0, SPAN), :] = result[i * SPAN : (i + 1) * SPAN]
            for i in range(GROUP // QUARTERS):
                rows = slice(i * HEAD_DIM, (i + 1) * HEAD_DIM)
                chosen = square_lane == index * (GROUP // QUARTERS) + i
                all_top = jnp.where(chosen, top[rows], all_top)
                all_total = jnp.where(chosen, total[rows], all_total)
        else:
            outs[0][here, :] = acc
            outs[1][here, :] = total
            outs[2][here, :] = top
    if last:
        log_total = jnp.transpose(all_top)[0:tiles] * SCALE
        log_total = log_total + jnp.log(jnp.transpose(all_total)[0:tiles])
        high = log_total.astype(jnp.bfloat16).astype(jnp.float32)
        low = log_total - high
        span = lax.axis_index("source") % SPANS
        kept = lane // SPAN == span
        for j in range(QUARTERS):
            shift = ((span - j) % QUARTERS) * SPAN
            terms = [jnp.where(kept, pltpu.roll(term, shift, 1), 0.0) for term in (high, low)]
            for i in range(tiles):
                extra = jnp.concatenate([term[i : i + 1, :] for term in terms], axis=0)
                place = rows_of(home(QUARTERS * i + j), BACK, SPAN, EXTRA)
                outs[0][place, :] = extra.astype(jnp.bfloat16)


def unpack_kernel(in_ref, out_ref, log_ref):
    log_totals = []
    for head in range(HEADS):
        terms = 0.0
        for span in range(SPANS):
            source = BACK_ORDER.index(SPANS * head + span)
            out_ref[
                span * SPAN : (span + 1) * SPAN, head * HEAD_DIM : (head + 1) * HEAD_DIM
            ] = in_ref[rows_of(source, BACK, 0, SPAN), :]
            terms += in_ref[rows_of(source, BACK, SPAN, EXTRA), :].astype(jnp.float32)
        log_totals.append(terms[0:1, :] + terms[1:2, :])
    log_ref[...] = jnp.concatenate(log_totals, axis=0)[:, 0 : SPANS * SPAN]


def params():
    return pltpu.CompilerParams(vmem_limit_bytes=VMEM_LIMIT)


def local(queries, keys, values, span_order):
    rows = queries.shape[0]
    devices = lax.axis_size("source")
    parts = devices // HEADS
    in_hbm = [
        pltpu.with_memory_space_constraint(array, pltpu.HBM)
        for array in (span_order, queries, keys, values)
    ]
    packed = pl.pallas_call(
        pack_kernel,
        out_shape=messages(THERE),
        in_specs=[HBM] * 4,
        out_specs=VMEM,
        scratch_shapes=[
            pltpu.SMEM(span_order.shape, jnp.int32),
            pltpu.VMEM((3,) + queries.shape, jnp.bfloat16),
            pltpu.SemaphoreType.DMA((4,)),
        ],
        compiler_params=params(),
    )(*in_hbm)
    mine = exchanged(packed, THERE_ORDER)
    total_rows = SOURCES * SPAN
    ring = [(i, i // parts * parts + (i + 1) % parts) for i in range(devices)]
    state = ()
    other = mine
    for part in range(parts):
        first, last = part == 0, part == parts - 1
        if last:
            shapes = (messages(BACK),)
            following = None
        else:
            shapes = (jax.ShapeDtypeStruct((total_rows, HEAD_DIM), jnp.float32),) * 3
            following = lax.ppermute(other, "source", ring)
        state = pl.pallas_call(
            functools.partial(attend_kernel, first, last),
            out_shape=shapes,
            in_specs=[VMEM] * (2 + len(state)),
            out_specs=(VMEM,) * len(shapes),
            compiler_params=params(),
            cost_estimate=pl.CostEstimate(
                flops=4 * total_rows * total_rows * HEAD_DIM,
                bytes_accessed=1 << 20,
                transcendentals=total_rows * total_rows,
            ),
        )(mine, other, *state)
        other = following
    back = exchanged(state[0], BACK_ORDER)
    return pl.pallas_call(
        unpack_kernel,
        out_shape=(
            jax.ShapeDtypeStruct((rows, HEADS * HEAD_DIM), jnp.bfloat16),
            jax.ShapeDtypeStruct((HEADS, rows), jnp.float32),
        ),
        in_specs=[VMEM],
        out_specs=(VMEM, VMEM),
        compiler_params=params(),
    )(back)


def solution(mesh):
    rows = P("source", None)
    return jax.shard_map(
        local,
        mesh=Mesh(mesh.devices.reshape(-1), ("source",)),
        in_specs=(rows, rows, rows, P("source")),
        out_specs=(rows, P(None, "source")),
        check_vma=False,
    )
```

```python
import functools
import math

import jax
import jax.numpy as jnp
from jax import lax
from jax.experimental import pallas as pl
from jax.experimental.pallas import tpu as pltpu
from jax.sharding import Mesh
from jax.sharding import PartitionSpec as P

HEADS = 16
HEAD_DIM = 128
SPAN = 32
DIGIT = 64
SPANS = 2
SOURCES = HEADS * SPANS
QUARTERS = HEAD_DIM // SPAN
EXTRA = 2
THERE = 3 * SPAN + EXTRA
BACK = SPAN + EXTRA
GROUP = 8
STEP = 8
THERE_ORDER = (
    0, 8, 16, 24, 2, 10, 18, 26, 1, 9, 17, 25, 3, 11, 19, 27, 4, 12, 20, 28, 6, 14, 22, 30, 5,
    13, 21, 29, 7, 15, 23, 31,
)
BACK_ORDER = (
    1, 31, 23, 15, 7, 29, 21, 13, 5, 30, 22, 0, 6, 28, 20, 12, 4, 27, 19, 11, 24, 26, 25, 14,
    9, 3, 18, 10, 17, 16, 8, 2,
)
MASKED = -1e30
SCALE = 1.0 / math.sqrt(HEAD_DIM)
SCALE2 = SCALE * math.log2(math.e)
VMEM_LIMIT = 48 * 1024 * 1024

VMEM = pl.BlockSpec(memory_space=pltpu.VMEM)
HBM = pl.BlockSpec(memory_space=pltpu.HBM)


def rows_of(message, size, first, count):
    return slice(message * size + first, message * size + first + count)


def messages(size):
    return jax.ShapeDtypeStruct((SOURCES * size, HEAD_DIM), jnp.bfloat16)


def exchanged(array, order):
    parts = lax.axis_size("source") // HEADS
    groups = [
        [member // SPANS * parts + first + member % SPANS for member in order]
        for first in range(0, parts, SPANS)
    ]
    paired = array.reshape(SOURCES, -1, 2, HEAD_DIM)
    paired = lax.all_to_all(paired, "source", 0, 0, axis_index_groups=groups, tiled=True)
    return paired.reshape(array.shape)


def pack_kernel(span_hbm, q_hbm, k_hbm, v_hbm, out_ref, ranks, buffers, sems):
    span_copy = pltpu.make_async_copy(span_hbm, ranks, sems.at[3])
    span_copy.start()
    copies = [
        pltpu.make_async_copy(source, buffers.at[i], sems.at[i])
        for i, source in enumerate((q_hbm, k_hbm, v_hbm))
    ]
    for copy in copies:
        copy.start()
    span_copy.wait()
    row = lax.broadcasted_iota(jnp.int32, (EXTRA, HEAD_DIM), 0)
    digits = []
    for span in range(SPANS):
        digit = jnp.where(row == 0, ranks[span] // DIGIT, ranks[span] % DIGIT)
        digits.append(digit.astype(jnp.float32).astype(jnp.bfloat16))
    for place, member in enumerate(THERE_ORDER):
        out_ref[rows_of(place, THERE, 3 * SPAN, EXTRA), :] = digits[member % SPANS]
    for i, copy in enumerate(copies):
        copy.wait()
        for place, member in enumerate(THERE_ORDER):
            head, span = member // SPANS, member % SPANS
            out_ref[rows_of(place, THERE, i * SPAN, SPAN), :] = buffers[
                i, span * SPAN : (span + 1) * SPAN, head * HEAD_DIM : (head + 1) * HEAD_DIM
            ]


def positions(ref):
    lane = lax.broadcasted_iota(jnp.int32, (EXTRA, HEAD_DIM), 1)
    ranks = []
    for i in range(0, SOURCES, QUARTERS):
        digits = 0.0
        for j in range(QUARTERS):
            extra = ref[rows_of(i + j, THERE, 3 * SPAN, EXTRA), :].astype(jnp.float32)
            digits = jnp.where(lane // SPAN == j, extra, digits)
        ranks.append(digits[0:1] * DIGIT + digits[1:2])
    rank = jnp.concatenate(ranks, axis=0)
    lane = lax.broadcasted_iota(jnp.int32, rank.shape, 1)
    return rank * SPAN + (lane % SPAN).astype(jnp.float32)


def spans(ref, sources, which):
    return jnp.concatenate(
        [ref[rows_of(source, THERE, which * SPAN, SPAN), :] for source in sources], axis=0
    )


def home(source):
    return BACK_ORDER.index(THERE_ORDER[source])


def attend_kernel(first, last, mine_ref, other_ref, *refs):
    if first:
        outs = refs
    else:
        acc_in, total_in, top_in, *outs = refs
    block = GROUP * SPAN
    blocks = SOURCES // GROUP
    tiles = SOURCES // QUARTERS
    keys = spans(other_ref, range(SOURCES), 1)
    key_pos = positions(other_ref)
    query_pos = key_pos if first else positions(mine_ref)
    key_tiles = [jnp.broadcast_to(key_pos[t : t + 1, :], (STEP, HEAD_DIM)) for t in range(tiles)]
    lane = lax.broadcasted_iota(jnp.int32, (STEP, HEAD_DIM), 1)
    row = lax.broadcasted_iota(jnp.int32, (STEP, HEAD_DIM), 0)

    def score(index):
        sources = range(index * GROUP, (index + 1) * GROUP)
        scores = lax.dot_general(
            spans(mine_ref, sources, 0),
            keys,
            (((1,), (1,)), ((), ())),
            preferred_element_type=jnp.float32,
        )
        masked = [[] for _ in range(tiles)]
        for i, source in enumerate(sources):
            tile, lead = source // QUARTERS, source % QUARTERS * SPAN
            start = query_pos[tile : tile + 1, lead : lead + 1]
            before = [key_tiles[t] < start for t in range(tiles)]
            for j in range(0, SPAN, STEP):
                here = i * SPAN + j
                for t in range(tiles):
                    visible = before[t]
                    if first and t == tile:
                        visible = visible | ((lane >= lead) & (lane - lead <= row + j))
                    piece = scores[here : here + STEP, t * HEAD_DIM : (t + 1) * HEAD_DIM]
                    masked[t].append(jnp.where(visible, piece, MASKED))
        masked = [jnp.concatenate(pieces, axis=0) for pieces in masked]
        return masked, jnp.max(functools.reduce(jnp.maximum, masked), axis=1, keepdims=True)

    following = score(0)
    values = spans(other_ref, range(SOURCES), 2)
    values = jnp.concatenate([values, jnp.ones_like(values)], axis=1)
    square_lane = lax.broadcasted_iota(jnp.int32, (HEAD_DIM, HEAD_DIM), 1)
    all_top = jnp.zeros((HEAD_DIM, HEAD_DIM), jnp.float32)
    all_total = jnp.ones((HEAD_DIM, HEAD_DIM), jnp.float32)
    for index in range(blocks):
        masked, top = following
        if index + 1 < blocks:
            following = score(index + 1)
        here = slice(index * block, (index + 1) * block)
        top = jnp.broadcast_to(top, (block, HEAD_DIM))
        if not first:
            old_top = top_in[here, :]
            top = jnp.maximum(top, old_top)
            factor = jnp.exp2((old_top - top) * SCALE2)
        weights = [jnp.exp2((piece - top) * SCALE2).astype(jnp.bfloat16) for piece in masked]
        summed = jnp.dot(
            jnp.concatenate(weights, axis=1), values, preferred_element_type=jnp.float32
        )
        acc, total = summed[:, :HEAD_DIM], summed[:, HEAD_DIM:]
        if not first:
            acc = acc + acc_in[here, :] * factor
            total = total + total_in[here, :] * factor
        if last:
            result = (acc * (1.0 / total)).astype(jnp.bfloat16)
            for i in range(GROUP):
                outs[0][rows_of(home(index * GROUP + i), BACK, 0, SPAN), :] = result[i * SPAN : (i + 1) * SPAN]
            for i in range(GROUP // QUARTERS):
                rows = slice(i * HEAD_DIM, (i + 1) * HEAD_DIM)
                chosen = square_lane == index * (GROUP // QUARTERS) + i
                all_top = jnp.where(chosen, top[rows], all_top)
                all_total = jnp.where(chosen, total[rows], all_total)
        else:
            outs[0][here, :] = acc
            outs[1][here, :] = total
            outs[2][here, :] = top
    if last:
        log_total = jnp.transpose(all_top)[0:tiles] * SCALE
        log_total = log_total + jnp.log(jnp.transpose(all_total)[0:tiles])
        high = log_total.astype(jnp.bfloat16).astype(jnp.float32)
        low = log_total - high
        span = lax.axis_index("source") % SPANS
        kept = lane // SPAN == span
        for j in range(QUARTERS):
            shift = ((span - j) % QUARTERS) * SPAN
            terms = [jnp.where(kept, pltpu.roll(term, shift, 1), 0.0) for term in (high, low)]
            for i in range(tiles):
                extra = jnp.concatenate([term[i : i + 1, :] for term in terms], axis=0)
                place = rows_of(home(QUARTERS * i + j), BACK, SPAN, EXTRA)
                outs[0][place, :] = extra.astype(jnp.bfloat16)


def unpack_kernel(in_ref, out_ref, log_ref):
    log_totals = []
    for head in range(HEADS):
        terms = 0.0
        for span in range(SPANS):
            source = BACK_ORDER.index(SPANS * head + span)
            out_ref[
                span * SPAN : (span + 1) * SPAN, head * HEAD_DIM : (head + 1) * HEAD_DIM
            ] = in_ref[rows_of(source, BACK, 0, SPAN), :]
            terms += in_ref[rows_of(source, BACK, SPAN, EXTRA), :].astype(jnp.float32)
        log_totals.append(terms[0:1, :] + terms[1:2, :])
    log_ref[...] = jnp.concatenate(log_totals, axis=0)[:, 0 : SPANS * SPAN]


def params():
    return pltpu.CompilerParams(vmem_limit_bytes=VMEM_LIMIT)


def local(queries, keys, values, span_order):
    rows = queries.shape[0]
    devices = lax.axis_size("source")
    parts = devices // HEADS
    in_hbm = [
        pltpu.with_memory_space_constraint(array, pltpu.HBM)
        for array in (span_order, queries, keys, values)
    ]
    packed = pl.pallas_call(
        pack_kernel,
        out_shape=messages(THERE),
        in_specs=[HBM] * 4,
        out_specs=VMEM,
        scratch_shapes=[
            pltpu.SMEM(span_order.shape, jnp.int32),
            pltpu.VMEM((3,) + queries.shape, jnp.bfloat16),
            pltpu.SemaphoreType.DMA((4,)),
        ],
        compiler_params=params(),
    )(*in_hbm)
    mine = exchanged(packed, THERE_ORDER)
    total_rows = SOURCES * SPAN
    ring = [(i, i // parts * parts + (i + 1) % parts) for i in range(devices)]
    state = ()
    other = mine
    for part in range(parts):
        first, last = part == 0, part == parts - 1
        if last:
            shapes = (messages(BACK),)
            following = None
        else:
            shapes = (jax.ShapeDtypeStruct((total_rows, HEAD_DIM), jnp.float32),) * 3
            following = lax.ppermute(other, "source", ring)
        state = pl.pallas_call(
            functools.partial(attend_kernel, first, last),
            out_shape=shapes,
            in_specs=[VMEM] * (2 + len(state)),
            out_specs=(VMEM,) * len(shapes),
            compiler_params=params(),
            cost_estimate=pl.CostEstimate(
                flops=4 * total_rows * total_rows * HEAD_DIM,
                bytes_accessed=1 << 20,
                transcendentals=total_rows * total_rows,
            ),
        )(mine, other, *state)
        other = following
    back = exchanged(state[0], BACK_ORDER)
    return pl.pallas_call(
        unpack_kernel,
        out_shape=(
            jax.ShapeDtypeStruct((rows, HEADS * HEAD_DIM), jnp.bfloat16),
            jax.ShapeDtypeStruct((HEADS, rows), jnp.float32),
        ),
        in_specs=[VMEM],
        out_specs=(VMEM, VMEM),
        compiler_params=params(),
    )(back)


def solution(mesh):
    rows = P("source", None)
    return jax.shard_map(
        local,
        mesh=Mesh(mesh.devices.reshape(-1), ("source",)),
        in_specs=(rows, rows, rows, P("source")),
        out_specs=(rows, P(None, "source")),
        check_vma=False,
    )
```

```python
import functools
import math

import jax
import jax.numpy as jnp
from jax import lax
from jax.experimental import pallas as pl
from jax.experimental.pallas import tpu as pltpu
from jax.sharding import Mesh
from jax.sharding import PartitionSpec as P

HEADS = 16
HEAD_DIM = 128
SPAN = 32
DIGIT = 64
SPANS = 2
SOURCES = HEADS * SPANS
QUARTERS = HEAD_DIM // SPAN
EXTRA = 2
THERE = 3 * SPAN + EXTRA
BACK = SPAN + EXTRA
KEYS = SOURCES * SPAN
GROUP = 16
STEP = 8
THERE_ORDER = (
    0, 8, 16, 24, 2, 10, 18, 26, 1, 9, 17, 25, 3, 11, 19, 27, 4, 12, 20, 28, 6, 14, 22, 30, 5,
    13, 21, 29, 7, 15, 23, 31,
)
BACK_ORDER = (
    1, 31, 23, 15, 7, 29, 21, 13, 5, 30, 22, 0, 6, 28, 20, 12, 4, 27, 19, 11, 24, 26, 25, 14,
    9, 3, 18, 10, 17, 16, 8, 2,
)
MASKED = -1e30
SCALE = 1.0 / math.sqrt(HEAD_DIM)
SCALE2 = SCALE * math.log2(math.e)
VMEM_LIMIT = 48 * 1024 * 1024

VMEM = pl.BlockSpec(memory_space=pltpu.VMEM)
HBM = pl.BlockSpec(memory_space=pltpu.HBM)


def rows_of(message, size, first, count):
    return slice(message * size + first, message * size + first + count)


def messages(size):
    return jax.ShapeDtypeStruct((SOURCES * size, HEAD_DIM), jnp.bfloat16)


def exchanged(array, order):
    parts = lax.axis_size("source") // HEADS
    groups = [
        [member // SPANS * parts + first + member % SPANS for member in order]
        for first in range(0, parts, SPANS)
    ]
    paired = array.reshape(SOURCES, -1, 2, HEAD_DIM)
    paired = lax.all_to_all(paired, "source", 0, 0, axis_index_groups=groups, tiled=True)
    return paired.reshape(array.shape)


def pack_kernel(span_hbm, q_hbm, k_hbm, v_hbm, out_ref, ranks, buffers, sems):
    span_copy = pltpu.make_async_copy(span_hbm, ranks, sems.at[3])
    span_copy.start()
    copies = [
        pltpu.make_async_copy(source, buffers.at[i], sems.at[i])
        for i, source in enumerate((q_hbm, k_hbm, v_hbm))
    ]
    for copy in copies:
        copy.start()
    span_copy.wait()
    row = lax.broadcasted_iota(jnp.int32, (EXTRA, HEAD_DIM), 0)
    digits = []
    for span in range(SPANS):
        digit = jnp.where(row == 0, ranks[span] // DIGIT, ranks[span] % DIGIT)
        digits.append(digit.astype(jnp.float32).astype(jnp.bfloat16))
    for place, member in enumerate(THERE_ORDER):
        out_ref[rows_of(place, THERE, 3 * SPAN, EXTRA), :] = digits[member % SPANS]
    for i, copy in enumerate(copies):
        copy.wait()
        for place, member in enumerate(THERE_ORDER):
            head, span = member // SPANS, member % SPANS
            out_ref[rows_of(place, THERE, i * SPAN, SPAN), :] = buffers[
                i, span * SPAN : (span + 1) * SPAN, head * HEAD_DIM : (head + 1) * HEAD_DIM
            ]


def sort_kernel(in_ref, queries_ref, others_ref):
    for source in range(SOURCES):
        for which, ref, start in ((1, others_ref, 0), (2, others_ref, KEYS), (0, queries_ref, 0)):
            place = rows_of(source, SPAN, start, SPAN)
            ref[place, :] = in_ref[rows_of(source, THERE, which * SPAN, SPAN), :]
        place = rows_of(source, EXTRA, 2 * KEYS, EXTRA)
        others_ref[place, :] = in_ref[rows_of(source, THERE, 3 * SPAN, EXTRA), :]


def positions(ref):
    lane = lax.broadcasted_iota(jnp.int32, (EXTRA, HEAD_DIM), 1)
    ranks = []
    for i in range(0, SOURCES, QUARTERS):
        digits = 0.0
        for j in range(QUARTERS):
            extra = ref[rows_of(i + j, EXTRA, 2 * KEYS, EXTRA), :].astype(jnp.float32)
            digits = jnp.where(lane // SPAN == j, extra, digits)
        ranks.append(digits[0:1] * DIGIT + digits[1:2])
    rank = jnp.concatenate(ranks, axis=0)
    lane = lax.broadcasted_iota(jnp.int32, rank.shape, 1)
    return rank * SPAN + (lane % SPAN).astype(jnp.float32)


def home(source):
    return BACK_ORDER.index(THERE_ORDER[source])


def attend_kernel(first, last, query_ref, mine_ref, other_ref, *refs):
    if first:
        outs = refs
    else:
        acc_in, total_in, top_in, *outs = refs
    block = GROUP * SPAN
    blocks = SOURCES // GROUP
    tiles = SOURCES // QUARTERS
    keys = other_ref[0:KEYS, :]
    key_pos = positions(other_ref)
    query_pos = key_pos if first else positions(mine_ref)
    key_tiles = [jnp.broadcast_to(key_pos[t : t + 1, :], (STEP, HEAD_DIM)) for t in range(tiles)]
    lane = lax.broadcasted_iota(jnp.int32, (STEP, HEAD_DIM), 1)
    row = lax.broadcasted_iota(jnp.int32, (STEP, HEAD_DIM), 0)

    def score(index):
        sources = range(index * GROUP, (index + 1) * GROUP)
        scores = lax.dot_general(
            query_ref[index * block : (index + 1) * block, :],
            keys,
            (((1,), (1,)), ((), ())),
            preferred_element_type=jnp.float32,
        )
        masked = [[] for _ in range(tiles)]
        for i, source in enumerate(sources):
            tile, lead = source // QUARTERS, source % QUARTERS * SPAN
            start = query_pos[tile : tile + 1, lead : lead + 1]
            before = [key_tiles[t] < start for t in range(tiles)]
            for j in range(0, SPAN, STEP):
                here = i * SPAN + j
                for t in range(tiles):
                    visible = before[t]
                    if first and t == tile:
                        visible = visible | ((lane >= lead) & (lane - lead <= row + j))
                    piece = scores[here : here + STEP, t * HEAD_DIM : (t + 1) * HEAD_DIM]
                    masked[t].append(jnp.where(visible, piece, MASKED))
        masked = [jnp.concatenate(pieces, axis=0) for pieces in masked]
        return masked, jnp.max(functools.reduce(jnp.maximum, masked), axis=1, keepdims=True)

    following = score(0)
    values = other_ref[KEYS : 2 * KEYS, :]
    values = jnp.concatenate([values, jnp.ones_like(values)], axis=1)
    square_lane = lax.broadcasted_iota(jnp.int32, (HEAD_DIM, HEAD_DIM), 1)
    all_top = jnp.zeros((HEAD_DIM, HEAD_DIM), jnp.float32)
    all_total = jnp.ones((HEAD_DIM, HEAD_DIM), jnp.float32)
    for index in range(blocks):
        masked, top = following
        if index + 1 < blocks:
            following = score(index + 1)
        here = slice(index * block, (index + 1) * block)
        top = jnp.broadcast_to(top, (block, HEAD_DIM))
        if not first:
            old_top = top_in[here, :]
            top = jnp.maximum(top, old_top)
            factor = jnp.exp2((old_top - top) * SCALE2)
        weights = [jnp.exp2((piece - top) * SCALE2).astype(jnp.bfloat16) for piece in masked]
        summed = jnp.dot(
            jnp.concatenate(weights, axis=1), values, preferred_element_type=jnp.float32
        )
        acc, total = summed[:, :HEAD_DIM], summed[:, HEAD_DIM:]
        if not first:
            acc = acc + acc_in[here, :] * factor
            total = total + total_in[here, :] * factor
        if last:
            result = (acc * (1.0 / total)).astype(jnp.bfloat16)
            for i in range(GROUP):
                outs[0][rows_of(home(index * GROUP + i), BACK, 0, SPAN), :] = result[i * SPAN : (i + 1) * SPAN]
            for i in range(GROUP // QUARTERS):
                rows = slice(i * HEAD_DIM, (i + 1) * HEAD_DIM)
                chosen = square_lane == index * (GROUP // QUARTERS) + i
                all_top = jnp.where(chosen, top[rows], all_top)
                all_total = jnp.where(chosen, total[rows], all_total)
        else:
            outs[0][here, :] = acc
            outs[1][here, :] = total
            outs[2][here, :] = top
    if last:
        log_total = jnp.transpose(all_top)[0:tiles] * SCALE
        log_total = log_total + jnp.log(jnp.transpose(all_total)[0:tiles])
        high = log_total.astype(jnp.bfloat16).astype(jnp.float32)
        low = log_total - high
        span = lax.axis_index("source") % SPANS
        kept = lane // SPAN == span
        for j in range(QUARTERS):
            shift = ((span - j) % QUARTERS) * SPAN
            terms = [jnp.where(kept, pltpu.roll(term, shift, 1), 0.0) for term in (high, low)]
            for i in range(tiles):
                extra = jnp.concatenate([term[i : i + 1, :] for term in terms], axis=0)
                place = rows_of(home(QUARTERS * i + j), BACK, SPAN, EXTRA)
                outs[0][place, :] = extra.astype(jnp.bfloat16)


def unpack_kernel(in_ref, out_ref, log_ref):
    log_totals = []
    for head in range(HEADS):
        terms = 0.0
        for span in range(SPANS):
            source = BACK_ORDER.index(SPANS * head + span)
            out_ref[
                span * SPAN : (span + 1) * SPAN, head * HEAD_DIM : (head + 1) * HEAD_DIM
            ] = in_ref[rows_of(source, BACK, 0, SPAN), :]
            terms += in_ref[rows_of(source, BACK, SPAN, EXTRA), :].astype(jnp.float32)
        log_totals.append(terms[0:1, :] + terms[1:2, :])
    log_ref[...] = jnp.concatenate(log_totals, axis=0)[:, 0 : SPANS * SPAN]


def params():
    return pltpu.CompilerParams(vmem_limit_bytes=VMEM_LIMIT)


def local(queries, keys, values, span_order):
    rows = queries.shape[0]
    devices = lax.axis_size("source")
    parts = devices // HEADS
    in_hbm = [
        pltpu.with_memory_space_constraint(array, pltpu.HBM)
        for array in (span_order, queries, keys, values)
    ]
    packed = pl.pallas_call(
        pack_kernel,
        out_shape=messages(THERE),
        in_specs=[HBM] * 4,
        out_specs=VMEM,
        scratch_shapes=[
            pltpu.SMEM(span_order.shape, jnp.int32),
            pltpu.VMEM((3,) + queries.shape, jnp.bfloat16),
            pltpu.SemaphoreType.DMA((4,)),
        ],
        compiler_params=params(),
    )(*in_hbm)
    queries, mine = pl.pallas_call(
        sort_kernel,
        out_shape=(
            jax.ShapeDtypeStruct((KEYS, HEAD_DIM), jnp.bfloat16),
            jax.ShapeDtypeStruct((2 * KEYS + SOURCES * EXTRA, HEAD_DIM), jnp.bfloat16),
        ),
        in_specs=[VMEM],
        out_specs=(VMEM, VMEM),
        compiler_params=params(),
    )(exchanged(packed, THERE_ORDER))
    ring = [(i, i // parts * parts + (i + 1) % parts) for i in range(devices)]
    state = ()
    other = mine
    for part in range(parts):
        first, last = part == 0, part == parts - 1
        if last:
            shapes = (messages(BACK),)
            following = None
        else:
            shapes = (jax.ShapeDtypeStruct((KEYS, HEAD_DIM), jnp.float32),) * 3
            following = lax.ppermute(other, "source", ring)
        state = pl.pallas_call(
            functools.partial(attend_kernel, first, last),
            out_shape=shapes,
            in_specs=[VMEM] * (3 + len(state)),
            out_specs=(VMEM,) * len(shapes),
            compiler_params=params(),
            cost_estimate=pl.CostEstimate(
                flops=4 * KEYS * KEYS * HEAD_DIM,
                bytes_accessed=1 << 20,
                transcendentals=KEYS * KEYS,
            ),
        )(queries, mine, other, *state)
        other = following
    back = exchanged(state[0], BACK_ORDER)
    return pl.pallas_call(
        unpack_kernel,
        out_shape=(
            jax.ShapeDtypeStruct((rows, HEADS * HEAD_DIM), jnp.bfloat16),
            jax.ShapeDtypeStruct((HEADS, rows), jnp.float32),
        ),
        in_specs=[VMEM],
        out_specs=(VMEM, VMEM),
        compiler_params=params(),
    )(back)


def solution(mesh):
    rows = P("source", None)
    return jax.shard_map(
        local,
        mesh=Mesh(mesh.devices.reshape(-1), ("source",)),
        in_specs=(rows, rows, rows, P("source")),
        out_specs=(rows, P(None, "source")),
        check_vma=False,
    )
```

```python
import functools
import math

import jax
import jax.numpy as jnp
from jax import lax
from jax.experimental import pallas as pl
from jax.experimental.pallas import tpu as pltpu
from jax.sharding import Mesh
from jax.sharding import PartitionSpec as P

HEADS = 16
HEAD_DIM = 128
SPAN = 32
DIGIT = 64
SPANS = 2
SOURCES = HEADS * SPANS
QUARTERS = HEAD_DIM // SPAN
EXTRA = 2
THERE = 3 * SPAN + EXTRA
BACK = SPAN + EXTRA
KEYS = SOURCES * SPAN
GROUP = 16
STEP = 8
THERE_ORDER = (
    0, 16, 24, 8, 10, 26, 18, 2, 1, 17, 25, 9, 11, 27, 19, 3, 4, 20, 28, 12, 14, 30, 22, 6, 5,
    21, 29, 13, 15, 31, 23, 7,
)
BACK_ORDER = (
    1, 31, 11, 15, 7, 29, 21, 30, 5, 13, 22, 0, 6, 28, 20, 12, 4, 27, 19, 23, 24, 26, 25, 14,
    9, 3, 18, 10, 17, 2, 8, 16,
)
MASKED = -1e30
SCALE = 1.0 / math.sqrt(HEAD_DIM)
SCALE2 = SCALE * math.log2(math.e)
VMEM_LIMIT = 48 * 1024 * 1024

VMEM = pl.BlockSpec(memory_space=pltpu.VMEM)
HBM = pl.BlockSpec(memory_space=pltpu.HBM)


def rows_of(message, size, first, count):
    return slice(message * size + first, message * size + first + count)


def messages(size):
    return jax.ShapeDtypeStruct((SOURCES * size, HEAD_DIM), jnp.bfloat16)


def exchanged(array, order):
    parts = lax.axis_size("source") // HEADS
    groups = [
        [member // SPANS * parts + first + member % SPANS for member in order]
        for first in range(0, parts, SPANS)
    ]
    paired = array.reshape(SOURCES, -1, 2, HEAD_DIM)
    paired = lax.all_to_all(paired, "source", 0, 0, axis_index_groups=groups, tiled=True)
    return paired.reshape(array.shape)


def pack_kernel(span_hbm, q_hbm, k_hbm, v_hbm, out_ref, ranks, buffers, sems):
    span_copy = pltpu.make_async_copy(span_hbm, ranks, sems.at[3])
    span_copy.start()
    copies = [
        pltpu.make_async_copy(source, buffers.at[i], sems.at[i])
        for i, source in enumerate((q_hbm, k_hbm, v_hbm))
    ]
    for copy in copies:
        copy.start()
    span_copy.wait()
    row = lax.broadcasted_iota(jnp.int32, (EXTRA, HEAD_DIM), 0)
    digits = []
    for span in range(SPANS):
        digit = jnp.where(row == 0, ranks[span] // DIGIT, ranks[span] % DIGIT)
        digits.append(digit.astype(jnp.float32).astype(jnp.bfloat16))
    for place, member in enumerate(THERE_ORDER):
        out_ref[rows_of(place, THERE, 3 * SPAN, EXTRA), :] = digits[member % SPANS]
    for i, copy in enumerate(copies):
        copy.wait()
        for place, member in enumerate(THERE_ORDER):
            head, span = member // SPANS, member % SPANS
            out_ref[rows_of(place, THERE, i * SPAN, SPAN), :] = buffers[
                i, span * SPAN : (span + 1) * SPAN, head * HEAD_DIM : (head + 1) * HEAD_DIM
            ]


def sort_kernel(in_ref, queries_ref, others_ref):
    for source in range(SOURCES):
        for which, ref, start in ((1, others_ref, 0), (2, others_ref, KEYS), (0, queries_ref, 0)):
            place = rows_of(source, SPAN, start, SPAN)
            ref[place, :] = in_ref[rows_of(source, THERE, which * SPAN, SPAN), :]
        place = rows_of(source, EXTRA, 2 * KEYS, EXTRA)
        others_ref[place, :] = in_ref[rows_of(source, THERE, 3 * SPAN, EXTRA), :]


def positions(ref):
    lane = lax.broadcasted_iota(jnp.int32, (EXTRA, HEAD_DIM), 1)
    ranks = []
    for i in range(0, SOURCES, QUARTERS):
        digits = 0.0
        for j in range(QUARTERS):
            extra = ref[rows_of(i + j, EXTRA, 2 * KEYS, EXTRA), :].astype(jnp.float32)
            digits = jnp.where(lane // SPAN == j, extra, digits)
        ranks.append(digits[0:1] * DIGIT + digits[1:2])
    rank = jnp.concatenate(ranks, axis=0)
    lane = lax.broadcasted_iota(jnp.int32, rank.shape, 1)
    return rank * SPAN + (lane % SPAN).astype(jnp.float32)


def home(source):
    return BACK_ORDER.index(THERE_ORDER[source])


def attend_kernel(first, last, query_ref, mine_ref, other_ref, *refs):
    if first:
        outs = refs
    else:
        acc_in, total_in, top_in, *outs = refs
    block = GROUP * SPAN
    blocks = SOURCES // GROUP
    tiles = SOURCES // QUARTERS
    keys = other_ref[0:KEYS, :]
    key_pos = positions(other_ref)
    query_pos = key_pos if first else positions(mine_ref)
    key_tiles = [jnp.broadcast_to(key_pos[t : t + 1, :], (STEP, HEAD_DIM)) for t in range(tiles)]
    lane = lax.broadcasted_iota(jnp.int32, (STEP, HEAD_DIM), 1)
    row = lax.broadcasted_iota(jnp.int32, (STEP, HEAD_DIM), 0)

    def score(index):
        sources = range(index * GROUP, (index + 1) * GROUP)
        scores = lax.dot_general(
            query_ref[index * block : (index + 1) * block, :],
            keys,
            (((1,), (1,)), ((), ())),
            preferred_element_type=jnp.float32,
        )
        masked = [[] for _ in range(tiles)]
        for i, source in enumerate(sources):
            tile, lead = source // QUARTERS, source % QUARTERS * SPAN
            start = query_pos[tile : tile + 1, lead : lead + 1]
            before = [key_tiles[t] < start for t in range(tiles)]
            for j in range(0, SPAN, STEP):
                here = i * SPAN + j
                for t in range(tiles):
                    visible = before[t]
                    if first and t == tile:
                        visible = visible | ((lane >= lead) & (lane - lead <= row + j))
                    piece = scores[here : here + STEP, t * HEAD_DIM : (t + 1) * HEAD_DIM]
                    masked[t].append(jnp.where(visible, piece, MASKED))
        masked = [jnp.concatenate(pieces, axis=0) for pieces in masked]
        return masked, jnp.max(functools.reduce(jnp.maximum, masked), axis=1, keepdims=True)

    following = score(0)
    values = other_ref[KEYS : 2 * KEYS, :]
    values = jnp.concatenate([values, jnp.ones_like(values)], axis=1)
    square_lane = lax.broadcasted_iota(jnp.int32, (HEAD_DIM, HEAD_DIM), 1)
    all_top = jnp.zeros((HEAD_DIM, HEAD_DIM), jnp.float32)
    all_total = jnp.ones((HEAD_DIM, HEAD_DIM), jnp.float32)
    for index in range(blocks):
        masked, top = following
        if index + 1 < blocks:
            following = score(index + 1)
        here = slice(index * block, (index + 1) * block)
        top = jnp.broadcast_to(top, (block, HEAD_DIM))
        if not first:
            old_top = top_in[here, :]
            top = jnp.maximum(top, old_top)
            factor = jnp.exp2((old_top - top) * SCALE2)
        weights = [jnp.exp2((piece - top) * SCALE2).astype(jnp.bfloat16) for piece in masked]
        summed = jnp.dot(
            jnp.concatenate(weights, axis=1), values, preferred_element_type=jnp.float32
        )
        acc, total = summed[:, :HEAD_DIM], summed[:, HEAD_DIM:]
        if not first:
            acc = acc + acc_in[here, :] * factor
            total = total + total_in[here, :] * factor
        if last:
            result = (acc * (1.0 / total)).astype(jnp.bfloat16)
            for i in range(GROUP):
                outs[0][rows_of(home(index * GROUP + i), BACK, 0, SPAN), :] = result[i * SPAN : (i + 1) * SPAN]
            for i in range(GROUP // QUARTERS):
                rows = slice(i * HEAD_DIM, (i + 1) * HEAD_DIM)
                chosen = square_lane == index * (GROUP // QUARTERS) + i
                all_top = jnp.where(chosen, top[rows], all_top)
                all_total = jnp.where(chosen, total[rows], all_total)
        else:
            outs[0][here, :] = acc
            outs[1][here, :] = total
            outs[2][here, :] = top
    if last:
        log_total = jnp.transpose(all_top)[0:tiles] * SCALE
        log_total = log_total + jnp.log(jnp.transpose(all_total)[0:tiles])
        high = log_total.astype(jnp.bfloat16).astype(jnp.float32)
        low = log_total - high
        span = lax.axis_index("source") % SPANS
        kept = lane // SPAN == span
        for j in range(QUARTERS):
            shift = ((span - j) % QUARTERS) * SPAN
            terms = [jnp.where(kept, pltpu.roll(term, shift, 1), 0.0) for term in (high, low)]
            for i in range(tiles):
                extra = jnp.concatenate([term[i : i + 1, :] for term in terms], axis=0)
                place = rows_of(home(QUARTERS * i + j), BACK, SPAN, EXTRA)
                outs[0][place, :] = extra.astype(jnp.bfloat16)


def unpack_kernel(in_ref, out_ref, log_ref):
    log_totals = []
    for head in range(HEADS):
        terms = 0.0
        for span in range(SPANS):
            source = BACK_ORDER.index(SPANS * head + span)
            out_ref[
                span * SPAN : (span + 1) * SPAN, head * HEAD_DIM : (head + 1) * HEAD_DIM
            ] = in_ref[rows_of(source, BACK, 0, SPAN), :]
            terms += in_ref[rows_of(source, BACK, SPAN, EXTRA), :].astype(jnp.float32)
        log_totals.append(terms[0:1, :] + terms[1:2, :])
    log_ref[...] = jnp.concatenate(log_totals, axis=0)[:, 0 : SPANS * SPAN]


def params():
    return pltpu.CompilerParams(vmem_limit_bytes=VMEM_LIMIT)


def local(queries, keys, values, span_order):
    rows = queries.shape[0]
    devices = lax.axis_size("source")
    parts = devices // HEADS
    in_hbm = [
        pltpu.with_memory_space_constraint(array, pltpu.HBM)
        for array in (span_order, queries, keys, values)
    ]
    packed = pl.pallas_call(
        pack_kernel,
        out_shape=messages(THERE),
        in_specs=[HBM] * 4,
        out_specs=VMEM,
        scratch_shapes=[
            pltpu.SMEM(span_order.shape, jnp.int32),
            pltpu.VMEM((3,) + queries.shape, jnp.bfloat16),
            pltpu.SemaphoreType.DMA((4,)),
        ],
        compiler_params=params(),
    )(*in_hbm)
    queries, mine = pl.pallas_call(
        sort_kernel,
        out_shape=(
            jax.ShapeDtypeStruct((KEYS, HEAD_DIM), jnp.bfloat16),
            jax.ShapeDtypeStruct((2 * KEYS + SOURCES * EXTRA, HEAD_DIM), jnp.bfloat16),
        ),
        in_specs=[VMEM],
        out_specs=(VMEM, VMEM),
        compiler_params=params(),
    )(exchanged(packed, THERE_ORDER))
    ring = [(i, i // parts * parts + (i + 1) % parts) for i in range(devices)]
    state = ()
    other = mine
    for part in range(parts):
        first, last = part == 0, part == parts - 1
        if last:
            shapes = (messages(BACK),)
            following = None
        else:
            shapes = (jax.ShapeDtypeStruct((KEYS, HEAD_DIM), jnp.float32),) * 3
            following = lax.ppermute(other, "source", ring)
        state = pl.pallas_call(
            functools.partial(attend_kernel, first, last),
            out_shape=shapes,
            in_specs=[VMEM] * (3 + len(state)),
            out_specs=(VMEM,) * len(shapes),
            compiler_params=params(),
            cost_estimate=pl.CostEstimate(
                flops=4 * KEYS * KEYS * HEAD_DIM,
                bytes_accessed=1 << 20,
                transcendentals=KEYS * KEYS,
            ),
        )(queries, mine, other, *state)
        other = following
    back = exchanged(state[0], BACK_ORDER)
    return pl.pallas_call(
        unpack_kernel,
        out_shape=(
            jax.ShapeDtypeStruct((rows, HEADS * HEAD_DIM), jnp.bfloat16),
            jax.ShapeDtypeStruct((HEADS, rows), jnp.float32),
        ),
        in_specs=[VMEM],
        out_specs=(VMEM, VMEM),
        compiler_params=params(),
    )(back)


def solution(mesh):
    rows = P("source", None)
    return jax.shard_map(
        local,
        mesh=Mesh(mesh.devices.reshape(-1), ("source",)),
        in_specs=(rows, rows, rows, P("source")),
        out_specs=(rows, P(None, "source")),
        check_vma=False,
    )
```

```python
import functools
import math

import jax
import jax.numpy as jnp
from jax import lax
from jax.experimental import pallas as pl
from jax.experimental.pallas import tpu as pltpu
from jax.sharding import Mesh
from jax.sharding import PartitionSpec as P

HEADS = 16
HEAD_DIM = 128
SPAN = 32
DIGIT = 64
SPANS = 2
SOURCES = HEADS * SPANS
QUARTERS = HEAD_DIM // SPAN
EXTRA = 2
THERE = 3 * SPAN + EXTRA
BACK = SPAN + EXTRA
KEYS = SOURCES * SPAN
GROUP = 16
STEP = 8
THERE_ORDER = (
    0, 16, 24, 8, 10, 26, 18, 2, 1, 17, 25, 9, 11, 27, 19, 3, 4, 20, 28, 12, 14, 30, 22, 6, 5,
    21, 29, 13, 15, 31, 23, 7,
)
BACK_ORDER = (
    1, 31, 11, 15, 7, 29, 21, 30, 5, 13, 22, 0, 6, 28, 20, 12, 4, 27, 19, 23, 24, 26, 25, 14,
    9, 3, 18, 10, 17, 2, 8, 16,
)
MASKED = -1e30
SCALE = 1.0 / math.sqrt(HEAD_DIM)
SCALE2 = SCALE * math.log2(math.e)
VMEM_LIMIT = 48 * 1024 * 1024

VMEM = pl.BlockSpec(memory_space=pltpu.VMEM)
HBM = pl.BlockSpec(memory_space=pltpu.HBM)


def rows_of(message, size, first, count):
    return slice(message * size + first, message * size + first + count)


def messages(size):
    return jax.ShapeDtypeStruct((SOURCES * size, HEAD_DIM), jnp.bfloat16)


def exchanged(array, order):
    parts = lax.axis_size("source") // HEADS
    groups = [
        [member // SPANS * parts + first + member % SPANS for member in order]
        for first in range(0, parts, SPANS)
    ]
    paired = array.reshape(SOURCES, -1, 2, HEAD_DIM)
    paired = lax.all_to_all(paired, "source", 0, 0, axis_index_groups=groups, tiled=True)
    return paired.reshape(array.shape)


def pack_kernel(span_hbm, q_hbm, k_hbm, v_hbm, out_ref, ranks, buffers, sems):
    span_copy = pltpu.make_async_copy(span_hbm, ranks, sems.at[3])
    span_copy.start()
    copies = [
        pltpu.make_async_copy(source, buffers.at[i], sems.at[i])
        for i, source in enumerate((q_hbm, k_hbm, v_hbm))
    ]
    for copy in copies:
        copy.start()
    span_copy.wait()
    row = lax.broadcasted_iota(jnp.int32, (EXTRA, HEAD_DIM), 0)
    digits = []
    for span in range(SPANS):
        digit = jnp.where(row == 0, ranks[span] // DIGIT, ranks[span] % DIGIT)
        digits.append(digit.astype(jnp.float32).astype(jnp.bfloat16))
    for place, member in enumerate(THERE_ORDER):
        out_ref[rows_of(place, THERE, 3 * SPAN, EXTRA), :] = digits[member % SPANS]
    for i, copy in enumerate(copies):
        copy.wait()
        for place, member in enumerate(THERE_ORDER):
            head, span = member // SPANS, member % SPANS
            out_ref[rows_of(place, THERE, i * SPAN, SPAN), :] = buffers[
                i, span * SPAN : (span + 1) * SPAN, head * HEAD_DIM : (head + 1) * HEAD_DIM
            ]


def sort_kernel(in_ref, others_ref):
    for source in range(SOURCES):
        for which, ref, start in ((1, others_ref, 0), (2, others_ref, KEYS)):
            place = rows_of(source, SPAN, start, SPAN)
            ref[place, :] = in_ref[rows_of(source, THERE, which * SPAN, SPAN), :]
        place = rows_of(source, EXTRA, 2 * KEYS, EXTRA)
        others_ref[place, :] = in_ref[rows_of(source, THERE, 3 * SPAN, EXTRA), :]


def positions(ref):
    lane = lax.broadcasted_iota(jnp.int32, (EXTRA, HEAD_DIM), 1)
    ranks = []
    for i in range(0, SOURCES, QUARTERS):
        digits = 0.0
        for j in range(QUARTERS):
            extra = ref[rows_of(i + j, EXTRA, 2 * KEYS, EXTRA), :].astype(jnp.float32)
            digits = jnp.where(lane // SPAN == j, extra, digits)
        ranks.append(digits[0:1] * DIGIT + digits[1:2])
    rank = jnp.concatenate(ranks, axis=0)
    lane = lax.broadcasted_iota(jnp.int32, rank.shape, 1)
    return rank * SPAN + (lane % SPAN).astype(jnp.float32)


def home(source):
    return BACK_ORDER.index(THERE_ORDER[source])


def attend_kernel(first, last, query_ref, mine_ref, other_ref, *refs):
    if first:
        outs = refs
    else:
        acc_in, total_in, top_in, *outs = refs
    block = GROUP * SPAN
    blocks = SOURCES // GROUP
    tiles = SOURCES // QUARTERS
    keys = other_ref[0:KEYS, :]
    key_pos = positions(other_ref)
    query_pos = key_pos if first else positions(mine_ref)
    key_tiles = [jnp.broadcast_to(key_pos[t : t + 1, :], (STEP, HEAD_DIM)) for t in range(tiles)]
    lane = lax.broadcasted_iota(jnp.int32, (STEP, HEAD_DIM), 1)
    row = lax.broadcasted_iota(jnp.int32, (STEP, HEAD_DIM), 0)

    def score(index):
        sources = range(index * GROUP, (index + 1) * GROUP)
        scores = lax.dot_general(
            jnp.concatenate([query_ref[rows_of(i, THERE, 0, SPAN), :] for i in sources], axis=0),
            keys,
            (((1,), (1,)), ((), ())),
            preferred_element_type=jnp.float32,
        )
        masked = [[] for _ in range(tiles)]
        for i, source in enumerate(sources):
            tile, lead = source // QUARTERS, source % QUARTERS * SPAN
            start = query_pos[tile : tile + 1, lead : lead + 1]
            before = [key_tiles[t] < start for t in range(tiles)]
            for j in range(0, SPAN, STEP):
                here = i * SPAN + j
                for t in range(tiles):
                    visible = before[t]
                    if first and t == tile:
                        visible = visible | ((lane >= lead) & (lane - lead <= row + j))
                    piece = scores[here : here + STEP, t * HEAD_DIM : (t + 1) * HEAD_DIM]
                    masked[t].append(jnp.where(visible, piece, MASKED))
        masked = [jnp.concatenate(pieces, axis=0) for pieces in masked]
        return masked, jnp.max(functools.reduce(jnp.maximum, masked), axis=1, keepdims=True)

    following = score(0)
    values = other_ref[KEYS : 2 * KEYS, :]
    values = jnp.concatenate([values, jnp.ones_like(values)], axis=1)
    square_lane = lax.broadcasted_iota(jnp.int32, (HEAD_DIM, HEAD_DIM), 1)
    all_top = jnp.zeros((HEAD_DIM, HEAD_DIM), jnp.float32)
    all_total = jnp.ones((HEAD_DIM, HEAD_DIM), jnp.float32)
    for index in range(blocks):
        masked, top = following
        if index + 1 < blocks:
            following = score(index + 1)
        here = slice(index * block, (index + 1) * block)
        top = jnp.broadcast_to(top, (block, HEAD_DIM))
        if not first:
            old_top = top_in[here, :]
            top = jnp.maximum(top, old_top)
            factor = jnp.exp2((old_top - top) * SCALE2)
        weights = [jnp.exp2((piece - top) * SCALE2).astype(jnp.bfloat16) for piece in masked]
        summed = jnp.dot(
            jnp.concatenate(weights, axis=1), values, preferred_element_type=jnp.float32
        )
        acc, total = summed[:, :HEAD_DIM], summed[:, HEAD_DIM:]
        if not first:
            acc = acc + acc_in[here, :] * factor
            total = total + total_in[here, :] * factor
        if last:
            result = (acc * (1.0 / total)).astype(jnp.bfloat16)
            for i in range(GROUP):
                outs[0][rows_of(home(index * GROUP + i), BACK, 0, SPAN), :] = result[i * SPAN : (i + 1) * SPAN]
            for i in range(GROUP // QUARTERS):
                rows = slice(i * HEAD_DIM, (i + 1) * HEAD_DIM)
                chosen = square_lane == index * (GROUP // QUARTERS) + i
                all_top = jnp.where(chosen, top[rows], all_top)
                all_total = jnp.where(chosen, total[rows], all_total)
        else:
            outs[0][here, :] = acc
            outs[1][here, :] = total
            outs[2][here, :] = top
    if last:
        log_total = jnp.transpose(all_top)[0:tiles] * SCALE
        log_total = log_total + jnp.log(jnp.transpose(all_total)[0:tiles])
        high = log_total.astype(jnp.bfloat16).astype(jnp.float32)
        low = log_total - high
        span = lax.axis_index("source") % SPANS
        kept = lane // SPAN == span
        for j in range(QUARTERS):
            shift = ((span - j) % QUARTERS) * SPAN
            terms = [jnp.where(kept, pltpu.roll(term, shift, 1), 0.0) for term in (high, low)]
            for i in range(tiles):
                extra = jnp.concatenate([term[i : i + 1, :] for term in terms], axis=0)
                place = rows_of(home(QUARTERS * i + j), BACK, SPAN, EXTRA)
                outs[0][place, :] = extra.astype(jnp.bfloat16)


def unpack_kernel(in_ref, out_ref, log_ref):
    log_totals = []
    for head in range(HEADS):
        terms = 0.0
        for span in range(SPANS):
            source = BACK_ORDER.index(SPANS * head + span)
            out_ref[
                span * SPAN : (span + 1) * SPAN, head * HEAD_DIM : (head + 1) * HEAD_DIM
            ] = in_ref[rows_of(source, BACK, 0, SPAN), :]
            terms += in_ref[rows_of(source, BACK, SPAN, EXTRA), :].astype(jnp.float32)
        log_totals.append(terms[0:1, :] + terms[1:2, :])
    log_ref[...] = jnp.concatenate(log_totals, axis=0)[:, 0 : SPANS * SPAN]


def params():
    return pltpu.CompilerParams(vmem_limit_bytes=VMEM_LIMIT)


def local(queries, keys, values, span_order):
    rows = queries.shape[0]
    devices = lax.axis_size("source")
    parts = devices // HEADS
    in_hbm = [
        pltpu.with_memory_space_constraint(array, pltpu.HBM)
        for array in (span_order, queries, keys, values)
    ]
    packed = pl.pallas_call(
        pack_kernel,
        out_shape=messages(THERE),
        in_specs=[HBM] * 4,
        out_specs=VMEM,
        scratch_shapes=[
            pltpu.SMEM(span_order.shape, jnp.int32),
            pltpu.VMEM((3,) + queries.shape, jnp.bfloat16),
            pltpu.SemaphoreType.DMA((4,)),
        ],
        compiler_params=params(),
    )(*in_hbm)
    queries = exchanged(packed, THERE_ORDER)
    mine = pl.pallas_call(
        sort_kernel,
        out_shape=jax.ShapeDtypeStruct((2 * KEYS + SOURCES * EXTRA, HEAD_DIM), jnp.bfloat16),
        in_specs=[VMEM],
        out_specs=VMEM,
        compiler_params=params(),
    )(queries)
    ring = [(i, i // parts * parts + (i + 1) % parts) for i in range(devices)]
    state = ()
    other = mine
    for part in range(parts):
        first, last = part == 0, part == parts - 1
        if last:
            shapes = (messages(BACK),)
            following = None
        else:
            shapes = (jax.ShapeDtypeStruct((KEYS, HEAD_DIM), jnp.float32),) * 3
            following = lax.ppermute(other, "source", ring)
        state = pl.pallas_call(
            functools.partial(attend_kernel, first, last),
            out_shape=shapes,
            in_specs=[VMEM] * (3 + len(state)),
            out_specs=(VMEM,) * len(shapes),
            compiler_params=params(),
            cost_estimate=pl.CostEstimate(
                flops=4 * KEYS * KEYS * HEAD_DIM,
                bytes_accessed=1 << 20,
                transcendentals=KEYS * KEYS,
            ),
        )(queries, mine, other, *state)
        other = following
    back = exchanged(state[0], BACK_ORDER)
    return pl.pallas_call(
        unpack_kernel,
        out_shape=(
            jax.ShapeDtypeStruct((rows, HEADS * HEAD_DIM), jnp.bfloat16),
            jax.ShapeDtypeStruct((HEADS, rows), jnp.float32),
        ),
        in_specs=[VMEM],
        out_specs=(VMEM, VMEM),
        compiler_params=params(),
    )(back)


def solution(mesh):
    rows = P("source", None)
    return jax.shard_map(
        local,
        mesh=Mesh(mesh.devices.reshape(-1), ("source",)),
        in_specs=(rows, rows, rows, P("source")),
        out_specs=(rows, P(None, "source")),
        check_vma=False,
    )
```
